512 devices in a mesh: dp: 8 (over z), ctx: 64 (over x, y, core).
Axes of the slice: x: 4, y: 8, z: 8, core: 2. Of those that a mesh axis runs over, the one named last changes fastest.
Arguments:
- tokens: bfloat16 [8, 8192, 1152], P('dp', 'ctx'), may hold values from -50 to 50
- cotangent: bfloat16 [8, 8192, 1152], P('dp', 'ctx'), may hold values from -45 to 45
- clip_frames: int32 [8, 8], P('dp'), may hold values from 1 to 32, as said below
- clip_offsets: int32 [8, 8], P('dp'), may hold values from 0 to 8064, as said below
- clip_heights: int32 [8, 8], P('dp'), may hold values from 8 to 16, as said below
- clip_widths: int32 [8, 8], P('dp'), may hold values from 4 to 8
- spatial_gain: float32 [1152], replicated, may hold values from 0.1 to 1.9
- spatial_qkv: bfloat16 [1728, 1152], P('ctx'), may hold values from -0.1875 to 0.1875
- spatial_out: bfloat16 [576, 1152], P('ctx'), may hold values from -0.25 to 0.25
- temporal_gain: float32 [1152], replicated, may hold values from 0.1 to 1.9
- temporal_qkv: bfloat16 [1728, 1152], P('ctx'), may hold values from -0.1875 to 0.1875
- temporal_out: bfloat16 [576, 1152], P('ctx'), may hold values from -0.25 to 0.25
Outputs:
- output: bfloat16 [8, 8192, 1152], P('dp', 'ctx')
- tokens_grad: bfloat16 [8, 8192, 1152], P('dp', 'ctx')
- gain_grads: float32 [2, 1152], replicated
The draws below stay inside these ranges and needn't reach their ends.
Inputs may be any that keep to these rules, and one draw needn't show every extreme that they name: `clip_frames`: clip 0 of every bin starts at offset 0 and has exactly 32 frame tiles; every later clip starts after the one before it ends, and the last ends by tile 64. `clip_offsets`: offsets are multiples of 128 and rise from clip to clip; the last clip of every bin starts at tile 64 - 1. `clip_heights`: clip 0 of every bin has 16 rows and 8 columns; heights times widths never exceed 128.
All inputs are finite; a program needn't handle non-finite values.
Results may differ from the reference program's by a relative error of at most 0.024.
Values may be sent and summed in bfloat16 or wider, within the bound.
A program may use at most 64 MiB of HBM per device.

```python
import math
import jax
import jax.numpy as jnp
from jax import lax

D = 1152
HEADS = 8
FRAME = 128
NCLIP = 8
INNER = 576
NF = 64
TOKENS = 8192
BINS = 8


def frame_layout(key):

    def one_bin(bin_key):
        cut_key, size_key = jax.random.split(bin_key)
        half_frames = NF // 2
        shuffled = jax.random.permutation(cut_key, half_frames - 2) + 1
        chosen = jnp.concatenate([shuffled[:NCLIP - 3], jnp.full((1,), half_frames - 1, jnp.int32)])
        cut_points = jnp.sort(chosen).astype(jnp.int32)
        boundaries = jnp.concatenate([jnp.zeros((1,), jnp.int32), cut_points, jnp.full((1,), half_frames, jnp.int32)])
        span_sizes = boundaries[1:] - boundaries[:-1]
        later_counts = jax.random.randint(size_key, (NCLIP - 1,), 1, span_sizes + 1).astype(jnp.int32)
        counts = jnp.concatenate([jnp.full((1,), half_frames, jnp.int32), later_counts])
        starts = jnp.concatenate([jnp.zeros((1,), jnp.int32), half_frames + boundaries[:-1]])
        return (counts, starts * FRAME)
    return jax.vmap(one_bin)(jax.random.split(key, BINS))


def draw_clip_frames(key, part):
    counts, starts = frame_layout(key)
    return counts


def draw_clip_offsets(key, part):
    counts, starts = frame_layout(key)
    return starts


def draw_clip_heights(key, part):
    key = jax.random.fold_in(key, 3)
    heights = jax.random.randint(key, (BINS, NCLIP), max(1, FRAME // 16), FRAME // 8 + 1).astype(jnp.int32)
    return heights.at[:, 0].set(FRAME // 8)


def draw_clip_widths(key, part):
    key = jax.random.fold_in(key, 4)
    widths_drawn = jax.random.randint(key, (BINS, NCLIP), 4, 9).astype(jnp.int32)
    return widths_drawn.at[:, 0].set(8)


def draw_tokens(key, part):
    key = jax.random.fold_in(key, 5)
    column_key, row_key, base_key = jax.random.split(key, 3)
    column_scale = jnp.exp(jax.random.uniform(column_key, (D,)) * math.log(10.0))
    row_scale = jnp.exp(jax.random.uniform(row_key, (BINS, TOKENS, 1)) * math.log(10.0))
    base_draw = jnp.clip(jax.random.normal(base_key, (BINS, TOKENS, D)), -5.0, 5.0)
    return (base_draw * column_scale * row_scale * 0.1).astype(jnp.bfloat16)


def draw_cotangent(key, part):
    key = jax.random.fold_in(key, 6)
    position = jnp.arange(TOKENS).astype(jnp.float32) / (TOKENS - 1)
    rising = (3.0 ** position)[None, :, None]
    base_draw = jnp.clip(jax.random.normal(key, (BINS, TOKENS, D)), -5.0, 5.0)
    return (base_draw * rising).astype(jnp.bfloat16)


def steps_of(rng, shape, shards, smallest, top_value):
    def one(dim, blocks):
        steps = jax.random.uniform(jax.random.fold_in(jax.random.fold_in(rng, 6), dim), (blocks,), jnp.float32, smallest / len(shards), top_value / len(shards))
        return jnp.repeat(jnp.exp(steps), shape[dim] // blocks).reshape((-1,) + (1,) * (len(shape) - dim - 1))

    factor_of = one(*shards[0])
    for cut in shards[1:]:
        factor_of = factor_of * one(*cut)
    return factor_of


def noise(stream_key, dims, scale, limit, pieces=(), kind=jnp.bfloat16):
    values = jax.random.normal(stream_key, dims, jnp.float32) * scale
    if len(pieces) > 0:
        values = steps_of(stream_key, dims, pieces, -0.22, 0.18) * values
    return jnp.clip(values, min=-limit, max=limit).astype(kind)


def setup_inputs(seed: int = 0) -> dict:
    keys = jax.random.split(jax.random.key(seed), 13)
    return {
        "tokens": draw_tokens(jax.random.fold_in(keys[12], 71), 0),
        "cotangent": draw_cotangent(jax.random.fold_in(keys[12], 71), 0),
        "clip_frames": draw_clip_frames(jax.random.fold_in(keys[12], 71), 0),
        "clip_offsets": draw_clip_offsets(jax.random.fold_in(keys[12], 71), 0),
        "clip_heights": draw_clip_heights(jax.random.fold_in(keys[12], 71), 0),
        "clip_widths": draw_clip_widths(jax.random.fold_in(keys[12], 71), 0),
        "spatial_gain": jnp.clip(1.0 + 0.18 * jax.random.normal(keys[6], (D,), jnp.float32), 0.1, 1.9),
        "spatial_qkv": noise(keys[7], (3 * INNER, D), D ** -0.5, 0.1875, ((0, 64),)),
        "spatial_out": noise(keys[8], (INNER, D), INNER ** -0.5, 0.25, ((0, 64),)),
        "temporal_gain": jnp.clip(1.0 + 0.18 * jax.random.normal(keys[9], (D,), jnp.float32), 0.1, 1.9),
        "temporal_qkv": noise(keys[10], (3 * INNER, D), D ** -0.5, 0.1875, ((0, 64),)),
        "temporal_out": noise(keys[11], (INNER, D), INNER ** -0.5, 0.25, ((0, 64),)),
    }


EPSILON = 1e-06
ROPE_BASE = 10000.0

def normalize(values, norm_gain):
    widened = values.astype(jnp.float32)
    mean_square = lax.optimization_barrier(jnp.mean(widened * widened, axis=-1, keepdims=True))
    return (widened * lax.rsqrt(mean_square + EPSILON) * norm_gain).astype(jnp.bfloat16)

def contract(left, right):
    return lax.dot_general(left, right, (((1,), (1,)), ((), ())), preferred_element_type=jnp.float32)

def attend(queries, keys_in, values, allowed, live_rows):
    score_scale = queries.shape[-1] ** (-0.5)
    scores = jnp.einsum('gqhe,gkhe->ghqk', queries.astype(jnp.float32), keys_in.astype(jnp.float32)) * score_scale
    weights = jnp.exp(scores) * allowed[:, None, :, :]
    totals = lax.optimization_barrier(jnp.sum(weights, axis=-1, keepdims=True)) + (1.0 - live_rows)[:, None, :, None]
    shares = (weights / totals).astype(jnp.bfloat16)
    blended = jnp.einsum('ghqk,gkhe->gqhe', shares.astype(jnp.float32), values.astype(jnp.float32))
    return (blended * live_rows[:, :, None, None]).astype(jnp.bfloat16)

def rotate(vectors, frame_times):
    half_size = vectors.shape[-1] // 2
    pair_index = jnp.arange(half_size).astype(jnp.float32)
    frequency = ROPE_BASE ** (-pair_index / half_size)
    angles = frame_times[:, None] * frequency[None, :]
    cosine_table = jnp.cos(angles)[None, :, None, :]
    sine_table = jnp.sin(angles)[None, :, None, :]
    widened = vectors.astype(jnp.float32)
    first_half = widened[..., :half_size]
    second_half = widened[..., half_size:]
    turned = jnp.concatenate([first_half * cosine_table - second_half * sine_table, first_half * sine_table + second_half * cosine_table], axis=-1)
    return turned.astype(jnp.bfloat16)

def clip_tables(clip_frames, clip_offsets, clip_heights, clip_widths, total_frames):
    starts = clip_offsets // FRAME
    frame_ids = jnp.arange(total_frames, dtype=jnp.int32)[:, None]
    member = ((frame_ids >= starts[None, :]) & (frame_ids < (starts + clip_frames)[None, :])).astype(jnp.float32)
    frame_times = lax.optimization_barrier(jnp.sum(member * (frame_ids - starts[None, :]).astype(jnp.float32), axis=1))
    counts = lax.optimization_barrier(jnp.sum(member * (clip_heights * clip_widths).astype(jnp.float32)[None, :], axis=1))
    same_clip = jnp.dot(member, member.T, precision=lax.Precision.HIGHEST)
    return (frame_times, counts, same_clip)

def spatial_block(tokens_in, norm_gain, project, output, allowed, live_rows):
    local_frames, frame_size, feature_count = tokens_in.shape
    normed = normalize(tokens_in, norm_gain)
    projected = contract(normed.reshape(-1, feature_count), project).astype(jnp.bfloat16)
    divided = projected.reshape(local_frames, frame_size, 3, HEADS, -1)
    blended = attend(divided[:, :, 0], divided[:, :, 1], divided[:, :, 2], allowed, live_rows)
    update = jnp.dot(blended.reshape(local_frames * frame_size, -1), output, preferred_element_type=jnp.float32)
    return (tokens_in.astype(jnp.float32) + update.reshape(tokens_in.shape)).astype(jnp.bfloat16)

def temporal_front(hidden, norm_gain, project):
    normed = normalize(hidden, norm_gain)
    projected = contract(normed.reshape(-1, normed.shape[-1]), project).astype(jnp.bfloat16)
    return projected.reshape(hidden.shape[:-1] + (project.shape[0],))

def temporal_core(projected, frame_times, allowed, live_rows):
    total_frames, slot_count = (projected.shape[0], projected.shape[1])
    divided = projected.reshape(total_frames, slot_count, 3, HEADS, -1)
    arranged = jnp.transpose(divided, (2, 1, 0, 3, 4))
    queries = rotate(arranged[0], frame_times)
    keys_in = rotate(arranged[1], frame_times)
    blended = attend(queries, keys_in, arranged[2], allowed, live_rows)
    return jnp.transpose(blended, (1, 0, 2, 3)).reshape(total_frames, slot_count, -1)

def temporal_back(hidden, blended, output):
    update = jnp.dot(blended.reshape(-1, blended.shape[-1]), output, preferred_element_type=jnp.float32)
    return (hidden.astype(jnp.float32) + update.reshape(hidden.shape)).astype(jnp.bfloat16)

def reference(tokens, cotangent, clip_frames, clip_offsets, clip_heights, clip_widths, spatial_gain, spatial_qkv, spatial_out, temporal_gain, temporal_qkv, temporal_out):

    def one_bin(bundle):
        tokens_bin, cotangent_bin, frames_bin, offsets_bin, heights_bin, widths_bin = bundle
        frame_times, counts, same_clip = clip_tables(frames_bin, offsets_bin, heights_bin, widths_bin, NF)
        slot_ids = jnp.arange(FRAME).astype(jnp.float32)
        live_space = (slot_ids[None, :] < counts[:, None]).astype(jnp.float32)
        allowed_space = jnp.broadcast_to(live_space[:, None, :], (NF, FRAME, FRAME))
        live_time = live_space.T
        allowed_time = same_clip[None, :, :] * live_time[:, None, :]

        def forward(tokens_in, space_gain, time_gain):
            hidden = spatial_block(tokens_in, space_gain, spatial_qkv, spatial_out, allowed_space, live_space)
            projected = temporal_front(hidden, time_gain, temporal_qkv)
            blended = temporal_core(projected, frame_times, allowed_time, live_time)
            return temporal_back(hidden, blended, temporal_out)
        result, pullback = jax.vjp(forward, tokens_bin.reshape(NF, FRAME, D), spatial_gain, temporal_gain)
        grad_tokens, grad_space, grad_time = pullback(cotangent_bin.reshape(NF, FRAME, D))
        return (result.reshape(TOKENS, D), grad_tokens.reshape(TOKENS, D), grad_space, grad_time)
    output, tokens_grad, grad_space, grad_time = lax.map(one_bin, (tokens, cotangent, clip_frames, clip_offsets, clip_heights, clip_widths))
    gain_grads = jnp.stack([lax.optimization_barrier(jnp.sum(grad_space, axis=0)), lax.optimization_barrier(jnp.sum(grad_time, axis=0))]) / math.sqrt(BINS * TOKENS)
    return (output, tokens_grad, gain_grads)
```

```python
import math

import jax
import jax.numpy as jnp
from jax import lax
from jax.experimental import pallas as pl
from jax.experimental.pallas import tpu as pltpu
from jax.sharding import PartitionSpec as P

HEADS = 8
FRAME = 128
LANES = 128
EPSILON = 1e-06
ROPE_BASE = 10000.0
HEAD_SIZE = 72
PIECE = 9
PIECE_PAD = 16
QKV_PAD = 32
GROUP = 256
GROUP_HEADS = 3 * LANES
HALF = 32
bf16 = jnp.bfloat16
f32 = jnp.float32
MESH = pl.DeviceIdType.MESH


def dot_nn(a, b):
    return lax.dot_general(a, b, (((1,), (0,)), ((), ())), preferred_element_type=f32)


def dot_nt(a, b):
    return lax.dot_general(a, b, (((1,), (1,)), ((), ())), preferred_element_type=f32)


def dot_tn(a, b):
    return lax.dot_general(a, b, (((0,), (0,)), ((), ())), preferred_element_type=f32)


def iota(shape, dim):
    return lax.broadcasted_iota(jnp.int32, shape, dim)


def spread_matrix():
    lane = iota((GROUP, GROUP_HEADS), 1)
    row = iota((GROUP, GROUP_HEADS), 0)
    block = lane >> 4
    within = lane & 15
    third = ((block * 11) >> 5)
    source = third * QKV_PAD + (block - 3 * third) * PIECE + within
    return jnp.where((row == source) & (within < PIECE), 1.0, 0.0).astype(bf16)


def normed_of(x, gain):
    r = lax.rsqrt(jnp.mean(x * x, axis=-1, keepdims=True) + EPSILON)
    return r, (x * r * gain).astype(bf16)


def norm_back(x, r, gain, dn):
    d_gain = jnp.sum(dn * (x * r), axis=0, keepdims=True)
    u = dn * gain
    inner = jnp.sum(u * x, axis=-1, keepdims=True) * (1.0 / x.shape[-1])
    return (r * u - x * (r * r * r * inner)).astype(bf16), d_gain


def project(normed, w_qkv, spread, put):
    for g in range(8):
        part = dot_nt(normed, w_qkv[g * GROUP : (g + 1) * GROUP, :]).astype(bf16)
        put(g * GROUP_HEADS, dot_nn(part, spread).astype(bf16))


def project_back(get, w_qkv, spread):
    parts = [
        dot_nt(get(g * GROUP_HEADS), spread).astype(bf16) for g in range(8)
    ]
    return dot_nn(jnp.concatenate(parts, axis=1), w_qkv[...])


SCALE = HEAD_SIZE ** (-0.5)


def share_of(q, k, mask, dead):
    w = jnp.where(mask, jnp.exp(dot_nt(q, k) * SCALE), 0.0)
    total = jnp.sum(w, axis=-1, keepdims=True) + dead
    return (w / total).astype(bf16)


def attend_back(q, k, v, share, g):
    dv = dot_tn(share, g).astype(bf16)
    ds = dot_nt(g, v).astype(bf16).astype(f32)
    p = share.astype(f32)
    c = jnp.sum(ds * p, axis=-1, keepdims=True)
    d = (p * (ds - c) * SCALE).astype(bf16)
    return dot_nn(d, k).astype(bf16), dot_tn(d, q).astype(bf16), dv


def head(h):
    return slice(h * LANES, (h + 1) * LANES)


def clip_scalars(frames, offsets, heights, widths):
    out = []
    for c in range(8):
        start = offsets[0, c] >> 7
        out.append((start, start + frames[0, c], heights[0, c] * widths[0, c]))
    return out


def space_forward(
    frames, offsets, heights, widths, tokens, gain, w_qkv, w_out, hidden_ref, slots_ref, qkv_ref, share_ref
):
    tile = lax.axis_index("ctx")
    count = jnp.int32(0)
    for first, last, size in clip_scalars(frames, offsets, heights, widths):
        count = count + jnp.where((tile >= first) & (tile < last), size, 0)
    x = tokens[0].astype(f32)
    r, normed = normed_of(x, gain[...])
    spread = spread_matrix()

    def put(lane, values):
        qkv_ref[:, lane : lane + GROUP_HEADS] = values

    project(normed, w_qkv, spread, put)
    live = jnp.where(iota((FRAME, 1), 0) < count, 1.0, 0.0)
    mask = iota((FRAME, FRAME), 1) < count
    blended = []
    for h in range(HEADS):
        share = share_of(qkv_ref[:, head(h)], qkv_ref[:, head(8 + h)], mask, 1.0 - live)
        share_ref[h] = share
        blended.append((dot_nn(share, qkv_ref[:, head(16 + h)]) * live).astype(bf16))
    update = dot_nn(jnp.concatenate(blended, axis=1), w_out[...])
    hidden = (x + update).astype(bf16)
    hidden_ref[...] = hidden
    slots_ref[...] = hidden.reshape(HALF, FRAME // HALF, hidden.shape[-1])


def cot_back(cotangent, w_out, out_ref):
    g = dot_nt(cotangent[0], w_out[...]).astype(bf16)
    out_ref[...] = g.reshape(HALF, FRAME // HALF, g.shape[-1])


def time_core(
    frames, offsets, heights, widths, hidden_ref, grad_ref, gain, w_qkv, blended_ref, front_ref, d_gain_ref, qkv_ref
):
    rank = lax.axis_index("ctx")
    base = (rank // HALF) * HALF
    slots = FRAME // HALF
    first_slot = lax.rem(rank, HALF) * slots
    clips = clip_scalars(frames, offsets, heights, widths)

    def tables(shape, dim):
        place = iota(shape, dim)
        tile = base + (place >> 2)
        slot = first_slot + (place & 3)
        ident = jnp.zeros(shape, jnp.int32)
        begin = jnp.zeros(shape, jnp.int32)
        count = jnp.zeros(shape, jnp.int32)
        for c, (first, last, size) in enumerate(clips):
            member = (tile >= first) & (tile < last)
            ident = jnp.where(member, c + 1, ident)
            begin = jnp.where(member, first, begin)
            count = jnp.where(member, size, count)
        time = jnp.where(ident > 0, tile - begin, 0)
        return ident * 4 + (place & 3), time.astype(f32), slot < count

    x = hidden_ref[...].astype(f32).reshape(FRAME, hidden_ref.shape[-1])
    r, normed = normed_of(x, gain[...])
    spread = spread_matrix()

    def put(lane, values):
        qkv_ref[:, lane : lane + GROUP_HEADS] = values

    project(normed, w_qkv, spread, put)
    key_q, time, live_q = tables((FRAME, 1), 0)
    key_k, _, live_k = tables((1, FRAME), 1)
    mask = (key_q == key_k) & live_k
    live = jnp.where(live_q, 1.0, 0.0)
    lane = iota((1, LANES), 1)
    pair = ((lane & 63) >> 4) * PIECE + (lane & 15)
    frequency = jnp.exp(pair.astype(f32) * (-math.log(ROPE_BASE) / (HEAD_SIZE // 2)))
    angle = time * frequency
    cosine = jnp.cos(angle)
    sine = jnp.where(lane < 64, -1.0, 1.0) * jnp.sin(angle)
    d_parts = [None] * 24
    blended = []
    grads = grad_ref[...].astype(f32).reshape(FRAME, grad_ref.shape[-1])
    for h in range(HEADS):
        q = qkv_ref[:, head(h)].astype(f32)
        k = qkv_ref[:, head(8 + h)].astype(f32)
        v = qkv_ref[:, head(16 + h)]
        q = (q * cosine + pltpu.roll(q, 64, 1) * sine).astype(bf16)
        k = (k * cosine + pltpu.roll(k, 64, 1) * sine).astype(bf16)
        share = share_of(q, k, mask, 1.0 - live)
        blended.append((dot_nn(share, v) * live).astype(bf16))
        dq, dk, dv = attend_back(q, k, v, share, (grads[:, head(h)] * live).astype(bf16))
        dq, dk = dq.astype(f32), dk.astype(f32)
        d_parts[h] = (dq * cosine - pltpu.roll(dq, 64, 1) * sine).astype(bf16)
        d_parts[8 + h] = (dk * cosine - pltpu.roll(dk, 64, 1) * sine).astype(bf16)
        d_parts[16 + h] = dv
    blended_ref[...] = jnp.concatenate(blended, axis=1).reshape(blended_ref.shape)
    for i in range(24):
        qkv_ref[:, head(i)] = d_parts[i]
    dn = project_back(lambda lane: qkv_ref[:, lane : lane + GROUP_HEADS], w_qkv, spread)
    front, d_gain = norm_back(x, r, gain[...], dn.astype(bf16).astype(f32))
    front_ref[...] = front.reshape(front_ref.shape)
    d_gain_ref[...] = d_gain


def space_back(
    frames,
    offsets,
    heights,
    widths,
    tokens,
    cotangent,
    hidden,
    blended_ref,
    front_ref,
    qkv_ref,
    share_ref,
    gain,
    w_qkv,
    w_out,
    w_time_out,
    out_ref,
    grad_ref,
    d_gain_ref,
    d_ref,
):
    tile = lax.axis_index("ctx")
    count = jnp.int32(0)
    for first, last, size in clip_scalars(frames, offsets, heights, widths):
        count = count + jnp.where((tile >= first) & (tile < last), size, 0)
    live = jnp.where(iota((FRAME, 1), 0) < count, 1.0, 0.0)
    spread = spread_matrix()
    blended = blended_ref[...].reshape(FRAME, blended_ref.shape[-1])
    out_ref[0] = (hidden[...].astype(f32) + dot_nn(blended, w_time_out[...])).astype(bf16)
    front = front_ref[...].astype(f32).reshape(FRAME, front_ref.shape[-1])
    d_hidden = (cotangent[0].astype(f32) + front).astype(bf16)
    d_blended = (dot_nt(d_hidden, w_out[...]).astype(bf16).astype(f32) * live).astype(bf16)
    for h in range(HEADS):
        dq, dk, dv = attend_back(
            qkv_ref[:, head(h)],
            qkv_ref[:, head(8 + h)],
            qkv_ref[:, head(16 + h)],
            share_ref[h],
            d_blended[:, head(h)],
        )
        d_ref[:, head(h)] = dq
        d_ref[:, head(8 + h)] = dk
        d_ref[:, head(16 + h)] = dv
    dn = project_back(lambda lane: d_ref[:, lane : lane + GROUP_HEADS], w_qkv, spread)
    x = tokens[0].astype(f32)
    r, _ = normed_of(x, gain[...])
    dx, d_gain = norm_back(x, r, gain[...], dn.astype(bf16).astype(f32))
    grad_ref[0] = (d_hidden.astype(f32) + dx.astype(f32)).astype(bf16)
    d_gain_ref[...] = d_gain


def exchange_kernel(n, collective, *refs):
    ins, outs = refs[:n], refs[n : 2 * n]
    send_sem, recv_sem, local_sem = refs[2 * n :]
    rank = lax.axis_index("ctx")
    plane = lax.axis_index("dp")
    base = (rank // HALF) * HALF
    me = rank - base
    barrier = pltpu.get_barrier_semaphore()

    def greet(step, carry):
        peer = base + lax.rem(me + step, HALF)
        pl.semaphore_signal(barrier, inc=1, device_id=(plane, peer), device_id_type=MESH)
        return carry

    lax.fori_loop(1, HALF, greet, 0)
    pl.semaphore_wait(barrier, HALF - 1)

    for i in range(n):
        src, dst = ins[i], outs[i]

        def send(step, carry):
            peer = lax.rem(me + step, HALF)
            pltpu.make_async_remote_copy(
                src_ref=src.at[peer],
                dst_ref=dst.at[me],
                send_sem=send_sem.at[i],
                recv_sem=recv_sem.at[i],
                device_id=(plane, base + peer),
                device_id_type=MESH,
            ).start()
            return carry

        lax.fori_loop(1, HALF, send, 0)
    copies = [
        pltpu.make_async_copy(ins[i].at[me], outs[i].at[me], local_sem.at[i]) for i in range(n)
    ]
    for c in copies:
        c.start()
    for c in copies:
        c.wait()
    for i in range(n):
        rest = pl.ds(0, HALF - 1)
        pltpu.make_async_copy(ins[i].at[rest], ins[i].at[rest], send_sem.at[i]).wait()
        pltpu.make_async_copy(outs[i].at[rest], outs[i].at[rest], recv_sem.at[i]).wait()


VMEM_SPEC = pl.BlockSpec(memory_space=pltpu.VMEM)
SMEM_SPEC = pl.BlockSpec(memory_space=pltpu.SMEM)
LIMIT = 48 * 1024 * 1024


def call(body, clips, operands, outs, scratch, flops=0):
    return pl.pallas_call(
        body,
        out_shape=outs,
        in_specs=[SMEM_SPEC] * len(clips) + [VMEM_SPEC] * len(operands),
        out_specs=[VMEM_SPEC] * len(outs),
        scratch_shapes=scratch,
        compiler_params=pltpu.CompilerParams(vmem_limit_bytes=LIMIT),
        cost_estimate=pl.CostEstimate(flops=flops, bytes_accessed=8 << 20, transcendentals=0),
    )(*clips, *operands)


def exchange(collective, *arrays):
    n = len(arrays)

    def body(*refs):
        exchange_kernel(n, collective, *refs)

    return pl.pallas_call(
        body,
        out_shape=[jax.ShapeDtypeStruct(a.shape, a.dtype) for a in arrays],
        in_specs=[VMEM_SPEC] * n,
        out_specs=[VMEM_SPEC] * n,
        scratch_shapes=[
            pltpu.SemaphoreType.DMA((n,)),
            pltpu.SemaphoreType.DMA((n,)),
            pltpu.SemaphoreType.DMA((n,)),
        ],
        compiler_params=pltpu.CompilerParams(
            collective_id=collective, has_side_effects=True, vmem_limit_bytes=LIMIT
        ),
    )(*arrays)


def gathered(shard, rows):
    padded = jnp.pad(shard, ((0, rows - shard.shape[0]), (0, 0)))
    return lax.all_gather(padded, "ctx", axis=0, tiled=True)


def shards(
    tokens,
    cotangent,
    clip_frames,
    clip_offsets,
    clip_heights,
    clip_widths,
    spatial_gain,
    spatial_qkv,
    spatial_out,
    temporal_gain,
    temporal_qkv,
    temporal_out,
):
    clips = (clip_frames, clip_offsets, clip_heights, clip_widths)
    width = tokens.shape[2]
    inner = HEADS * LANES
    w_qkv = gathered(spatial_qkv, QKV_PAD)
    w_out = gathered(spatial_out, PIECE_PAD)
    w_time_out = gathered(temporal_out, PIECE_PAD)
    w_time_qkv = gathered(temporal_qkv, QKV_PAD)
    space_gain = spatial_gain.reshape(1, width)
    time_gain = temporal_gain.reshape(1, width)
    slots = FRAME // HALF

    def out(*shape, dtype=bf16):
        return jax.ShapeDtypeStruct(shape, dtype)

    hidden, hidden_slabs, qkv, share = call(
        space_forward,
        clips,
        (tokens, space_gain, w_qkv, w_out),
        [out(FRAME, width), out(HALF, slots, width), out(FRAME, 3 * inner), out(HEADS, FRAME, FRAME)],
        [],
    )
    (grad_slabs,) = call(
        cot_back, (), (cotangent, w_time_out), [out(HALF, slots, inner)], []
    )
    hidden_slots, grad_slots = exchange(0, hidden_slabs, grad_slabs)
    blended_slots, front_slots, time_gain_part = call(
        time_core,
        clips,
        (hidden_slots, grad_slots, time_gain, w_time_qkv),
        [out(HALF, slots, inner), out(HALF, slots, width), out(1, width, dtype=f32)],
        [pltpu.VMEM((FRAME, 3 * inner), bf16)],
    )
    blended, front = exchange(1, blended_slots, front_slots)
    result, grad_tokens, space_gain_part = call(
        space_back,
        clips,
        (
            tokens,
            cotangent,
            hidden,
            blended,
            front,
            qkv,
            share,
            space_gain,
            w_qkv,
            w_out,
            w_time_out,
        ),
        [out(1, FRAME, width), out(1, FRAME, width), out(1, width, dtype=f32)],
        [pltpu.VMEM((FRAME, 3 * inner), bf16)],
    )
    total = lax.psum(jnp.concatenate([space_gain_part, time_gain_part], axis=0), ("dp", "ctx"))
    bins = lax.axis_size("dp")
    tiles = lax.axis_size("ctx")
    return result, grad_tokens, total * (1.0 / math.sqrt(bins * tiles * FRAME))


def solution(mesh):
    return jax.shard_map(
        shards,
        mesh=mesh,
        in_specs=(
            P("dp", "ctx", None),
            P("dp", "ctx", None),
            P("dp", None),
            P("dp", None),
            P("dp", None),
            P("dp", None),
            P(),
            P("ctx", None),
            P("ctx", None),
            P(),
            P("ctx", None),
            P("ctx", None),
        ),
        out_specs=(P("dp", "ctx", None), P("dp", "ctx", None), P()),
        check_vma=False,
    )
```

```python
import math

import jax
import jax.numpy as jnp
from jax import lax
from jax.experimental import pallas as pl
from jax.experimental.pallas import tpu as pltpu
from jax.sharding import PartitionSpec as P

HEADS = 8
FRAME = 128
LANES = 128
EPSILON = 1e-06
ROPE_BASE = 10000.0
HEAD_SIZE = 72
PIECE = 9
PIECE_PAD = 16
QKV_PAD = 32
GROUP = 256
GROUP_HEADS = 3 * LANES
HALF = 32
bf16 = jnp.bfloat16
f32 = jnp.float32
MESH = pl.DeviceIdType.MESH


def dot_nn(a, b):
    return lax.dot_general(a, b, (((1,), (0,)), ((), ())), preferred_element_type=f32)


def dot_nt(a, b):
    return lax.dot_general(a, b, (((1,), (1,)), ((), ())), preferred_element_type=f32)


def dot_tn(a, b):
    return lax.dot_general(a, b, (((0,), (0,)), ((), ())), preferred_element_type=f32)


def iota(shape, dim):
    return lax.broadcasted_iota(jnp.int32, shape, dim)


def spread_matrix():
    lane = iota((GROUP, GROUP_HEADS), 1)
    row = iota((GROUP, GROUP_HEADS), 0)
    block = lane >> 4
    within = lane & 15
    third = ((block * 11) >> 5)
    source = third * QKV_PAD + (block - 3 * third) * PIECE + within
    return jnp.where((row == source) & (within < PIECE), 1.0, 0.0).astype(bf16)


def normed_of(x, gain):
    r = lax.rsqrt(jnp.mean(x * x, axis=-1, keepdims=True) + EPSILON)
    return r, (x * r * gain).astype(bf16)


def norm_back(x, r, gain, dn):
    d_gain = jnp.sum(dn * (x * r), axis=0, keepdims=True)
    u = dn * gain
    inner = jnp.sum(u * x, axis=-1, keepdims=True) * (1.0 / x.shape[-1])
    return (r * u - x * (r * r * r * inner)).astype(bf16), d_gain


def qkv_rows(weights, g):
    half = slice(8 * (g % 2), 8 * (g % 2) + 8)
    return weights[g // 2, half, 0:2].reshape(GROUP, weights.shape[-1])


def project(normed, weights, spread, into, g):
    part = dot_nt(normed, qkv_rows(weights, g)).astype(bf16)
    into[:, g * GROUP_HEADS : (g + 1) * GROUP_HEADS] = dot_nn(part, spread).astype(bf16)


def project_back(grads, weights, spread):
    parts = [
        dot_nt(grads[:, g * GROUP_HEADS : (g + 1) * GROUP_HEADS], spread).astype(bf16) for g in range(8)
    ]
    rows = weights[:, :, 0:2].reshape(8 * GROUP, weights.shape[-1])
    return dot_nn(jnp.concatenate(parts, axis=1), rows)


def out_rows(weights):
    return weights[:, :, 2].reshape(HEADS * LANES, weights.shape[-1])


SCALE = HEAD_SIZE ** (-0.5)


def share_of(q, k, mask, dead):
    w = jnp.where(mask, jnp.exp(dot_nt(q, k) * SCALE), 0.0)
    total = jnp.sum(w, axis=-1, keepdims=True) + dead
    return (w / total).astype(bf16)


def attend_back(q, k, v, share, g):
    dv = dot_tn(share, g).astype(bf16)
    ds = dot_nt(g, v).astype(bf16).astype(f32)
    p = share.astype(f32)
    c = jnp.sum(ds * p, axis=-1, keepdims=True)
    d = (p * (ds - c) * SCALE).astype(bf16)
    return dot_nn(d, k).astype(bf16), dot_tn(d, q).astype(bf16), dv


def head(h):
    return slice(h * LANES, (h + 1) * LANES)


def clip_scalars(frames, offsets, heights, widths):
    out = []
    for c in range(8):
        start = offsets[0, c] >> 7
        out.append((start, start + frames[0, c], heights[0, c] * widths[0, c]))
    return out


XS, YS, CORES = 4, 8, 2
SLOTS = FRAME // HALF


def wait_bytes(ref, sem):
    pltpu.make_async_copy(ref, ref, sem).wait()


class Place:
    def __init__(self):
        self.plane = lax.axis_index("dp")
        self.planes = lax.axis_size("dp")
        self.rank = lax.axis_index("ctx")
        self.x = self.rank // (YS * CORES)
        self.y = lax.rem(self.rank // CORES, YS)
        self.core = lax.rem(self.rank, CORES)

    def device(self, x=None, y=None, core=None, plane=None):
        x = self.x if x is None else x
        y = self.y if y is None else y
        core = self.core if core is None else core
        plane = self.plane if plane is None else plane
        return (plane, (x * YS + y) * CORES + core)

    def dx(self, step):
        return lax.rem(self.x + step + XS, XS)

    def dy(self, step):
        return lax.rem(self.y + step + YS, YS)

    def dz(self, step):
        return lax.rem(self.plane + step + self.planes, self.planes)


def gather_steps(at, weights, sems):
    (y_recv, x_recv, z_recv, sib_recv, y_send, x_send, z_send, sib_send) = sems
    mine = 1 - lax.rem(at.plane, 2)
    other = 1 - mine
    steps = []

    def add(time, action):
        steps.append((time, len(steps), action))

    def block(x, y, piece):
        return weights.at[x, y * CORES + at.core, piece]

    def send(ref, device, send_sem, recv_sem):
        pltpu.make_async_remote_copy(
            src_ref=ref, dst_ref=ref, send_sem=send_sem, recv_sem=recv_sem, device_id=device, device_id_type=MESH
        ).start()

    def sibling(y, piece, group):
        send(
            weights.at[:, y * CORES + at.core, piece],
            at.device(core=1 - at.core),
            sib_send.at[group],
            sib_recv.at[group],
        )

    up, down = at.device(y=at.dy(1)), at.device(y=at.dy(-1))
    right, left = at.device(x=at.dx(1)), at.device(x=at.dx(-1))
    above, below = at.device(plane=at.dz(1)), at.device(plane=at.dz(-1))

    def y_of(j):
        return at.dy(-j) if j <= 4 else at.dy(j - 4)

    def ident(kind, j):
        return j - 1 if kind == 0 else 7 + (kind - 1) * 8 + j

    def x_of(kind):
        return (at.x, at.dx(-1), at.dx(1), at.dx(2))[kind]

    def over_z(kind, j):
        i = ident(kind, j)
        send(block(x_of(kind), y_of(j), mine), above if i % 2 == 0 else below, z_send.at[i % 2], z_recv.at[i])

    plus = (0, 1, 2, 3)

    def arrive_y(j):
        ref = block(at.x, y_of(j), mine)
        if j > 0:
            wait_bytes(ref, y_recv.at[ident(0, j)])
        if j in (0, 1, 2, 3):
            send(ref, up, y_send.at[0], y_recv.at[ident(0, j + 1)])
        if j in (0, 5, 6):
            send(ref, down, y_send.at[0], y_recv.at[ident(0, 5 if j == 0 else j + 1)])
        send(ref, right, y_send.at[1], y_recv.at[ident(1, j)])
        send(ref, left, y_send.at[1], y_recv.at[ident(2, j)])
        if j > 0:
            over_z(0, j)

    def arrive_x(kind, j):
        ref = block(x_of(kind), y_of(j), mine)
        wait_bytes(ref, y_recv.at[ident(kind, j)])
        if kind == 1 and j in plus:
            send(ref, right, y_send.at[1], y_recv.at[ident(3, j)])
        if kind == 2 and j not in plus:
            send(ref, left, y_send.at[1], y_recv.at[ident(3, j)])
        over_z(kind, j)

    def arrive_z(j):
        for kind in range(4):
            if kind > 0 or j > 0:
                wait_bytes(block(x_of(kind), y_of(j), other), z_recv.at[ident(kind, j)])
        sibling(y_of(j), other, 2)

    for j in range(8):
        far = j if j <= 4 else j - 4
        add(far, lambda j=j: arrive_y(j))
        for kind in (1, 2, 3):
            add(far + (1 if kind < 3 else 2), lambda kind=kind, j=j: arrive_x(kind, j))
        add(far + 3, lambda j=j: sibling(y_of(j), mine, 0))
        add(far + 4, lambda j=j: arrive_z(j))

    def y_at(j):
        return at.dy(-j) if j <= 3 else at.dy(j - 3)

    def number(kind, j):
        return kind - 1 if j == 0 else 3 + kind * 7 + j - 1

    def come(kind, j):
        ref = block(x_of(kind), y_at(j), 2)
        if kind > 0 or j > 0:
            wait_bytes(ref, x_recv.at[number(kind, j)])
        if j == 0 and kind == 0:
            send(ref, right, x_send.at[0], x_recv.at[number(1, 0)])
            send(ref, left, x_send.at[0], x_recv.at[number(2, 0)])
        if j == 0 and kind == 2:
            send(ref, left, x_send.at[0], x_recv.at[number(3, 0)])
        if j in (0, 1, 2):
            send(ref, up, x_send.at[1], x_recv.at[number(kind, j + 1)])
        if j in (0, 4, 5, 6):
            send(ref, down, x_send.at[1], x_recv.at[number(kind, 4 if j == 0 else j + 1)])

    for j in range(8):
        far = j if j <= 3 else j - 3
        for kind in range(4):
            add(far + (0, 1, 1, 2)[kind], lambda kind=kind, j=j: come(kind, j))
        add(far + 3, lambda j=j: sibling(y_at(j), 2, 1))

    def finish(group):
        wait_bytes(weights.at[:, 0:8, 0], sib_recv.at[group])

    def drain():
        wait_bytes(weights.at[0, 0:7, 0], y_send.at[0])
        wait_bytes(weights.at[0:3, 0:8, 0], y_send.at[1])
        wait_bytes(weights.at[0, 0:3, 0], x_send.at[0])
        wait_bytes(weights.at[:, 0:7, 0], x_send.at[1])
        wait_bytes(weights.at[0, 0:16, 0], z_send.at[0])
        wait_bytes(weights.at[0, 0:15, 0], z_send.at[1])
        for group in range(3):
            wait_bytes(weights.at[:, 0:8, 0], sib_send.at[group])

    by_time = [[a for _, _, a in sorted(s for s in steps if s[0] == t)] for t in range(9)]
    return by_time, finish, drain


def whole(
    frames,
    offsets,
    heights,
    widths,
    tokens,
    cotangent,
    space_gain,
    space_qkv,
    space_out,
    time_gain,
    time_qkv,
    time_out,
    out_ref,
    grad_ref,
    gains_ref,
    space_w,
    time_w,
    qkv,
    time_q,
    share,
    time_share,
    hidden_ref,
    hidden_out,
    hidden_in,
    back_out,
    back_in,
    blend_out,
    blend_in,
    front_out,
    front_in,
    sums,
    sums_x,
    sums_y,
    sums_z,
    *sems,
):
    space_sems, time_sems = sems[0:8], sems[8:16]
    slab_send, slab_recv, slab_own, sum_send, sum_recv = sems[16:]
    at = Place()
    rank, plane = at.rank, at.plane
    base = (rank // HALF) * HALF
    me = rank - base

    barrier = pltpu.get_barrier_semaphore()

    def greet(device):
        pl.semaphore_signal(barrier, inc=1, device_id=device, device_id_type=MESH)

    def greet_half(step, carry):
        greet((plane, base + lax.rem(me + step, HALF)))
        return carry

    column = at.x * CORES + at.core

    def on_x(i):
        return at.device(x=i // CORES, core=lax.rem(i, CORES))

    def greet_x(step, carry):
        greet(on_x(lax.rem(column + step, XS * CORES)))
        return carry

    def greet_z(step, carry):
        greet(at.device(plane=lax.rem(plane + step, at.planes)))
        return carry

    lax.fori_loop(1, HALF, greet_half, 0)
    lax.fori_loop(1, XS * CORES, greet_x, 0)
    lax.fori_loop(1, at.planes, greet_z, 0)

    for weights, shard_qkv, shard_out in ((space_w, space_qkv, space_out), (time_w, time_qkv, time_out)):
        own = weights.at[at.x, at.y * CORES + at.core]
        width = shard_qkv.shape[-1]
        own[0] = shard_qkv[0:16, :]
        own[1] = jnp.concatenate(
            [shard_qkv[16:27, :].astype(f32), jnp.zeros((5, width), f32)], axis=0
        ).astype(bf16)
        own[2] = jnp.concatenate([shard_out[...].astype(f32), jnp.zeros((7, width), f32)], axis=0).astype(bf16)

    pl.semaphore_wait(barrier, HALF - 1 + XS * CORES - 1 + at.planes - 1)

    space_steps, space_finish, space_drain = gather_steps(at, space_w, space_sems)
    time_steps, time_finish, time_drain = gather_steps(at, time_w, time_sems)

    def run(actions):
        for action in actions:
            action()

    def slabs_start(i, src, dst):
        def step(k, carry):
            peer = lax.rem(me + k, HALF)
            pltpu.make_async_remote_copy(
                src_ref=src.at[peer],
                dst_ref=dst.at[me],
                send_sem=slab_send.at[i],
                recv_sem=slab_recv.at[i],
                device_id=(plane, base + peer),
                device_id_type=MESH,
            ).start()
            return carry

        lax.fori_loop(1, HALF, step, 0)
        own = pltpu.make_async_copy(src.at[me], dst.at[me], slab_own.at[i])
        own.start()
        own.wait()

    def slabs_wait(i, dst):
        wait_bytes(dst.at[pl.ds(0, HALF - 1)], slab_recv.at[i])

    def slabs_drain(i, src):
        wait_bytes(src.at[pl.ds(0, HALF - 1)], slab_send.at[i])

    clips = clip_scalars(frames, offsets, heights, widths)
    spread = spread_matrix()

    run(space_steps[0])
    x = tokens[0].astype(f32)
    _, normed = normed_of(x, space_gain[...])
    for t in range(1, 9):
        run(space_steps[t])
    for group in range(3):
        space_finish(group)
    run(time_steps[0])
    count = jnp.int32(0)
    for first, last, size in clips:
        count = count + jnp.where((rank >= first) & (rank < last), size, 0)
    live_space = jnp.where(iota((FRAME, 1), 0) < count, 1.0, 0.0)
    mask_space = iota((FRAME, FRAME), 1) < count
    for g in range(8):
        project(normed, space_w, spread, qkv, g)
        if g % 2 == 1:
            run(time_steps[1 + g // 2])
    blended = []
    for h in range(HEADS):
        s = share_of(qkv[:, head(h)], qkv[:, head(8 + h)], mask_space, 1.0 - live_space)
        share[h] = s
        blended.append((dot_nn(s, qkv[:, head(16 + h)]) * live_space).astype(bf16))
        if h % 2 == 1:
            run(time_steps[5 + h // 2])
    hidden = (x + dot_nn(jnp.concatenate(blended, axis=1), out_rows(space_w))).astype(bf16)
    hidden_ref[...] = hidden
    hidden_out[...] = hidden.reshape(hidden_out.shape)
    slabs_start(0, hidden_out, hidden_in)
    time_finish(1)
    back = dot_nt(cotangent[0], out_rows(time_w)).astype(bf16)
    back_out[...] = back.reshape(back_out.shape)
    slabs_start(1, back_out, back_in)

    def tables(shape, dim):
        place = iota(shape, dim)
        tile = base + (place >> 2)
        slot = me * SLOTS + (place & 3)
        ident = jnp.zeros(shape, jnp.int32)
        begin = jnp.zeros(shape, jnp.int32)
        size_of = jnp.zeros(shape, jnp.int32)
        for c, (first, last, size) in enumerate(clips):
            member = (tile >= first) & (tile < last)
            ident = jnp.where(member, c + 1, ident)
            begin = jnp.where(member, first, begin)
            size_of = jnp.where(member, size, size_of)
        time = jnp.where(ident > 0, tile - begin, 0)
        return ident * 4 + (place & 3), time.astype(f32), slot < size_of

    key_q, time, live_q = tables((FRAME, 1), 0)
    key_k, _, live_k = tables((1, FRAME), 1)
    mask = (key_q == key_k) & live_k
    live = jnp.where(live_q, 1.0, 0.0)
    lane = iota((1, LANES), 1)
    pair = ((lane & 63) >> 4) * PIECE + (lane & 15)
    frequency = jnp.exp(pair.astype(f32) * (-math.log(ROPE_BASE) / (HEAD_SIZE // 2)))
    angle = time * frequency
    cosine = jnp.cos(angle)
    sine = jnp.where(lane < 64, -1.0, 1.0) * jnp.sin(angle)

    time_finish(0)
    time_finish(2)
    slabs_wait(0, hidden_in)
    x_time = hidden_in[...].astype(f32).reshape(FRAME, hidden_in.shape[-1])
    r_time, normed = normed_of(x_time, time_gain[...])
    for g in range(8):
        project(normed, time_w, spread, time_q, g)
    blended = []
    for h in range(HEADS):
        q = time_q[:, head(h)].astype(f32)
        k = time_q[:, head(8 + h)].astype(f32)
        q = (q * cosine + pltpu.roll(q, 64, 1) * sine).astype(bf16)
        k = (k * cosine + pltpu.roll(k, 64, 1) * sine).astype(bf16)
        time_q[:, head(h)] = q
        time_q[:, head(8 + h)] = k
        s = share_of(q, k, mask, 1.0 - live)
        time_share[h] = s
        blended.append((dot_nn(s, time_q[:, head(16 + h)]) * live).astype(bf16))
    blend_out[...] = jnp.concatenate(blended, axis=1).reshape(blend_out.shape)
    slabs_start(2, blend_out, blend_in)
    slabs_wait(1, back_in)
    grads = back_in[...].astype(f32).reshape(FRAME, back_in.shape[-1]) * live
    for h in range(HEADS):
        dq, dk, dv = attend_back(
            time_q[:, head(h)],
            time_q[:, head(8 + h)],
            time_q[:, head(16 + h)],
            time_share[h],
            grads[:, head(h)].astype(bf16),
        )
        dq, dk = dq.astype(f32), dk.astype(f32)
        time_q[:, head(h)] = (dq * cosine - pltpu.roll(dq, 64, 1) * sine).astype(bf16)
        time_q[:, head(8 + h)] = (dk * cosine - pltpu.roll(dk, 64, 1) * sine).astype(bf16)
        time_q[:, head(16 + h)] = dv
    dn = project_back(time_q, time_w, spread).astype(bf16).astype(f32)
    front, d_time_gain = norm_back(x_time, r_time, time_gain[...], dn)
    front_out[...] = front.reshape(front_out.shape)
    slabs_start(3, front_out, front_in)

    slabs_wait(2, blend_in)
    blended = blend_in[...].reshape(FRAME, blend_in.shape[-1])
    out_ref[0] = (hidden_ref[...].astype(f32) + dot_nn(blended, out_rows(time_w))).astype(bf16)

    slabs_wait(3, front_in)
    front = front_in[...].astype(f32).reshape(FRAME, front_in.shape[-1])
    d_hidden = (cotangent[0].astype(f32) + front).astype(bf16)
    d_blended = (dot_nt(d_hidden, out_rows(space_w)).astype(bf16).astype(f32) * live_space).astype(bf16)
    for h in range(HEADS):
        dq, dk, dv = attend_back(
            qkv[:, head(h)], qkv[:, head(8 + h)], qkv[:, head(16 + h)], share[h], d_blended[:, head(h)]
        )
        qkv[:, head(h)] = dq
        qkv[:, head(8 + h)] = dk
        qkv[:, head(16 + h)] = dv
    dn = project_back(qkv, space_w, spread).astype(bf16).astype(f32)
    x = tokens[0].astype(f32)
    r, _ = normed_of(x, space_gain[...])
    dx, d_space_gain = norm_back(x, r, space_gain[...], dn)

    def reduce(i, size, mine, held, to):
        held[mine] = sums[...]

        def step(k, carry):
            pltpu.make_async_remote_copy(
                src_ref=sums,
                dst_ref=held.at[mine],
                send_sem=sum_send.at[i],
                recv_sem=sum_recv.at[i],
                device_id=to(lax.rem(mine + k, size)),
                device_id_type=MESH,
            ).start()
            return carry

        lax.fori_loop(1, size, step, 0)

    def reduced(i, size, held):
        if size > 1:
            wait_bytes(held.at[pl.ds(0, size - 1)], sum_recv.at[i])
            wait_bytes(held.at[pl.ds(0, size - 1)], sum_send.at[i])
        total = held[0]
        for k in range(1, size):
            total = total + held[k]
        return total

    sums[0:1] = d_space_gain
    sums[1:2] = d_time_gain
    reduce(0, XS * CORES, column, sums_x, on_x)
    grad_ref[0] = (d_hidden.astype(f32) + dx.astype(f32)).astype(bf16)
    total = reduced(0, XS * CORES, sums_x)
    sums[...] = total
    reduce(1, YS, at.y, sums_y, lambda i: at.device(y=i))
    for i, src in ((0, hidden_out), (1, back_out), (2, blend_out), (3, front_out)):
        slabs_drain(i, src)
    total = reduced(1, YS, sums_y)
    sums[...] = total
    reduce(2, at.planes, plane, sums_z, lambda i: at.device(plane=i))
    space_drain()
    time_drain()
    total = reduced(2, at.planes, sums_z)
    gains_ref[...] = total * (1.0 / math.sqrt(at.planes * XS * YS * CORES * FRAME))


VMEM_SPEC = pl.BlockSpec(memory_space=pltpu.VMEM)
SMEM_SPEC = pl.BlockSpec(memory_space=pltpu.SMEM)
LIMIT = 56 * 1024 * 1024


def shards(
    tokens,
    cotangent,
    clip_frames,
    clip_offsets,
    clip_heights,
    clip_widths,
    spatial_gain,
    spatial_qkv,
    spatial_out,
    temporal_gain,
    temporal_qkv,
    temporal_out,
):
    width = tokens.shape[2]
    inner = HEADS * LANES
    planes = lax.axis_size("dp")
    dma = pltpu.SemaphoreType.DMA

    def slab(columns):
        return pltpu.VMEM((HALF, SLOTS, columns), bf16)

    gather_sems = [dma((31,)), dma((31,)), dma((31,)), dma((3,)), dma((2,)), dma((2,)), dma((2,)), dma((3,))]
    return pl.pallas_call(
        whole,
        out_shape=[
            jax.ShapeDtypeStruct(tokens.shape, bf16),
            jax.ShapeDtypeStruct(tokens.shape, bf16),
            jax.ShapeDtypeStruct((2, width), f32),
        ],
        in_specs=[SMEM_SPEC] * 4 + [VMEM_SPEC] * 8,
        out_specs=[VMEM_SPEC] * 3,
        scratch_shapes=[
            pltpu.VMEM((XS, YS * CORES, 3, 16, width), bf16),
            pltpu.VMEM((XS, YS * CORES, 3, 16, width), bf16),
            pltpu.VMEM((FRAME, 3 * inner), bf16),
            pltpu.VMEM((FRAME, 3 * inner), bf16),
            pltpu.VMEM((HEADS, FRAME, FRAME), bf16),
            pltpu.VMEM((HEADS, FRAME, FRAME), bf16),
            pltpu.VMEM((FRAME, width), bf16),
            slab(width),
            slab(width),
            slab(inner),
            slab(inner),
            slab(inner),
            slab(inner),
            slab(width),
            slab(width),
            pltpu.VMEM((2, width), f32),
            pltpu.VMEM((XS * CORES, 2, width), f32),
            pltpu.VMEM((YS, 2, width), f32),
            pltpu.VMEM((planes, 2, width), f32),
        ]
        + gather_sems
        + gather_sems
        + [dma((4,)), dma((4,)), dma((4,)), dma((3,)), dma((3,))],
        compiler_params=pltpu.CompilerParams(
            collective_id=0, has_side_effects=True, vmem_limit_bytes=LIMIT
        ),
    )(
        clip_frames,
        clip_offsets,
        clip_heights,
        clip_widths,
        tokens,
        cotangent,
        spatial_gain.reshape(1, width),
        spatial_qkv,
        spatial_out,
        temporal_gain.reshape(1, width),
        temporal_qkv,
        temporal_out,
    )


def solution(mesh):
    return jax.shard_map(
        shards,
        mesh=mesh,
        in_specs=(
            P("dp", "ctx", None),
            P("dp", "ctx", None),
            P("dp", None),
            P("dp", None),
            P("dp", None),
            P("dp", None),
            P(),
            P("ctx", None),
            P("ctx", None),
            P(),
            P("ctx", None),
            P("ctx", None),
        ),
        out_specs=(P("dp", "ctx", None), P("dp", "ctx", None), P()),
        check_vma=False,
    )
```

```python
import math

import jax
import jax.numpy as jnp
from jax import lax
from jax.experimental import pallas as pl
from jax.experimental.pallas import tpu as pltpu
from jax.sharding import PartitionSpec as P

HEADS = 8
FRAME = 128
LANES = 128
EPSILON = 1e-06
ROPE_BASE = 10000.0
HEAD_SIZE = 72
PIECE = 9
PIECE_PAD = 16
QKV_PAD = 32
GROUP = 256
GROUP_HEADS = 3 * LANES
HALF = 32
bf16 = jnp.bfloat16
f32 = jnp.float32
MESH = pl.DeviceIdType.MESH


def dot_nn(a, b):
    return lax.dot_general(a, b, (((1,), (0,)), ((), ())), preferred_element_type=f32)


def dot_nt(a, b):
    return lax.dot_general(a, b, (((1,), (1,)), ((), ())), preferred_element_type=f32)


def dot_tn(a, b):
    return lax.dot_general(a, b, (((0,), (0,)), ((), ())), preferred_element_type=f32)


def iota(shape, dim):
    return lax.broadcasted_iota(jnp.int32, shape, dim)


def spread_matrix():
    lane = iota((GROUP, GROUP_HEADS), 1)
    row = iota((GROUP, GROUP_HEADS), 0)
    block = lane >> 4
    within = lane & 15
    third = ((block * 11) >> 5)
    source = third * QKV_PAD + (block - 3 * third) * PIECE + within
    return jnp.where((row == source) & (within < PIECE), 1.0, 0.0).astype(bf16)


def normed_of(x, gain):
    r = lax.rsqrt(jnp.mean(x * x, axis=-1, keepdims=True) + EPSILON)
    return r, (x * r * gain).astype(bf16)


def norm_back(x, r, gain, dn):
    d_gain = jnp.sum(dn * (x * r), axis=0, keepdims=True)
    u = dn * gain
    inner = jnp.sum(u * x, axis=-1, keepdims=True) * (1.0 / x.shape[-1])
    return (r * u - x * (r * r * r * inner)).astype(bf16), d_gain


def qkv_rows(weights, g):
    half = slice(8 * (g % 2), 8 * (g % 2) + 8)
    return weights[g // 2, half, 0:2].reshape(GROUP, weights.shape[-1])


def project(normed, weights, spread, into, g):
    part = dot_nt(normed, qkv_rows(weights, g)).astype(bf16)
    into[:, g * GROUP_HEADS : (g + 1) * GROUP_HEADS] = dot_nn(part, spread).astype(bf16)


def project_back(grads, weights, spread):
    parts = [
        dot_nt(grads[:, g * GROUP_HEADS : (g + 1) * GROUP_HEADS], spread).astype(bf16) for g in range(8)
    ]
    rows = weights[:, :, 0:2].reshape(8 * GROUP, weights.shape[-1])
    return dot_nn(jnp.concatenate(parts, axis=1), rows)


def out_rows(weights):
    return weights[:, :, 2].reshape(HEADS * LANES, weights.shape[-1])


SCALE = HEAD_SIZE ** (-0.5)


def share_of(q, k, mask, dead):
    w = jnp.where(mask, jnp.exp(dot_nt(q, k) * SCALE), 0.0)
    total = jnp.sum(w, axis=-1, keepdims=True) + dead
    return (w / total).astype(bf16)


def attend_back(q, k, v, share, g):
    dv = dot_tn(share, g).astype(bf16)
    ds = dot_nt(g, v).astype(bf16).astype(f32)
    p = share.astype(f32)
    c = jnp.sum(ds * p, axis=-1, keepdims=True)
    d = (p * (ds - c) * SCALE).astype(bf16)
    return dot_nn(d, k).astype(bf16), dot_tn(d, q).astype(bf16), dv


def head(h):
    return slice(h * LANES, (h + 1) * LANES)


def clip_scalars(frames, offsets, heights, widths):
    out = []
    for c in range(8):
        start = offsets[0, c] >> 7
        out.append((start, start + frames[0, c], heights[0, c] * widths[0, c]))
    return out


XS, YS, CORES = 4, 8, 2
SPACE_DONE, TIME_AFTER = 8, 5
SLOTS = FRAME // HALF


def wait_bytes(ref, sem):
    pltpu.make_async_copy(ref, ref, sem).wait()


def gain_row(gain):
    return gain[...].reshape(1, gain.shape[0])


class Place:
    def __init__(self):
        self.plane = lax.axis_index("dp")
        self.planes = lax.axis_size("dp")
        self.rank = lax.axis_index("ctx")
        self.x = self.rank // (YS * CORES)
        self.y = lax.rem(self.rank // CORES, YS)
        self.core = lax.rem(self.rank, CORES)

    def device(self, x=None, y=None, core=None, plane=None):
        x = self.x if x is None else x
        y = self.y if y is None else y
        core = self.core if core is None else core
        plane = self.plane if plane is None else plane
        return (plane, (x * YS + y) * CORES + core)

    def dx(self, step):
        return lax.rem(self.x + step + XS, XS)

    def dy(self, step):
        return lax.rem(self.y + step + YS, YS)

    def dz(self, step):
        return lax.rem(self.plane + step + self.planes, self.planes)


class Gather:
    def __init__(self, at, weights):
        self.at = at
        self.weights = weights
        self.up, self.down = at.device(y=at.dy(1)), at.device(y=at.dy(-1))
        self.right, self.left = at.device(x=at.dx(1)), at.device(x=at.dx(-1))
        self.above, self.below = at.device(plane=at.dz(1)), at.device(plane=at.dz(-1))

    def block(self, x, y, piece):
        return self.weights.at[x, y * CORES + self.at.core, piece]

    def x_of(self, kind):
        return (self.at.x, self.at.dx(-1), self.at.dx(1), self.at.dx(2))[kind]

    def send(self, ref, device, send_sem, recv_sem):
        pltpu.make_async_remote_copy(
            src_ref=ref, dst_ref=ref, send_sem=send_sem, recv_sem=recv_sem, device_id=device, device_id_type=MESH
        ).start()

    def sibling(self, y, piece, sems):
        at = self.at
        ref = self.weights.at[:, y * CORES + at.core, piece]
        self.send(ref, at.device(core=1 - at.core), sems[0], sems[1])

    def sibling_wait(self, sem):
        wait_bytes(self.weights.at[:, 0:8, 0], sem)

    def y_first(self, piece, recv, sent, sib, other=None, z_recv=None, z_sent=None, z_sib=None):
        at = self.at
        steps = []

        def y_of(j):
            return at.dy(-j) if j <= 4 else at.dy(j - 4)

        def ident(kind, j):
            return j - 1 if kind == 0 else 7 + (kind - 1) * 8 + j

        def over_z(kind, j):
            if other is not None:
                i = ident(kind, j)
                ref = self.block(self.x_of(kind), y_of(j), piece)
                self.send(ref, self.above if i % 2 == 0 else self.below, z_sent.at[i % 2], z_recv.at[i])

        plus = (0, 1, 2, 3)

        def arrive_y(j):
            ref = self.block(at.x, y_of(j), piece)
            if j > 0:
                wait_bytes(ref, recv.at[ident(0, j)])
            if j in (0, 1, 2, 3):
                self.send(ref, self.up, sent.at[0], recv.at[ident(0, j + 1)])
            if j in (0, 5, 6):
                self.send(ref, self.down, sent.at[0], recv.at[ident(0, 5 if j == 0 else j + 1)])
            self.send(ref, self.right, sent.at[1], recv.at[ident(1, j)])
            self.send(ref, self.left, sent.at[1], recv.at[ident(2, j)])
            if j > 0:
                over_z(0, j)

        def arrive_x(kind, j):
            ref = self.block(self.x_of(kind), y_of(j), piece)
            wait_bytes(ref, recv.at[ident(kind, j)])
            if kind == 1 and j in plus:
                self.send(ref, self.right, sent.at[1], recv.at[ident(3, j)])
            if kind == 2 and j not in plus:
                self.send(ref, self.left, sent.at[1], recv.at[ident(3, j)])
            over_z(kind, j)

        def arrive_z(j):
            for kind in range(4):
                if kind > 0 or j > 0:
                    wait_bytes(self.block(self.x_of(kind), y_of(j), other), z_recv.at[ident(kind, j)])
            self.sibling(y_of(j), other, z_sib)

        for j in range(8):
            far = j if j <= 4 else j - 4
            steps.append((far, lambda j=j: arrive_y(j)))
            for kind in (1, 2, 3):
                steps.append((far + (1 if kind < 3 else 2), lambda kind=kind, j=j: arrive_x(kind, j)))
            steps.append((far + 2, lambda j=j: self.sibling(y_of(j), piece, sib)))
            if other is not None:
                steps.append((far + 3, lambda j=j: arrive_z(j)))
        return steps

    def y_first_drain(self, sent, z_sent=None):
        wait_bytes(self.weights.at[0, 0:7, 0], sent.at[0])
        wait_bytes(self.weights.at[0:3, 0:8, 0], sent.at[1])
        if z_sent is not None:
            wait_bytes(self.weights.at[0, 0:16, 0], z_sent.at[0])
            wait_bytes(self.weights.at[0, 0:15, 0], z_sent.at[1])

    def x_first(self, piece, recv, sent, sib):
        at = self.at
        steps = []

        def y_of(j):
            return at.dy(-j) if j <= 3 else at.dy(j - 3)

        def number(kind, j):
            return kind - 1 if j == 0 else 3 + kind * 7 + j - 1

        def come(kind, j):
            ref = self.block(self.x_of(kind), y_of(j), piece)
            if kind > 0 or j > 0:
                wait_bytes(ref, recv.at[number(kind, j)])
            if j == 0 and kind == 0:
                self.send(ref, self.right, sent.at[0], recv.at[number(1, 0)])
                self.send(ref, self.left, sent.at[0], recv.at[number(2, 0)])
            if j == 0 and kind == 2:
                self.send(ref, self.left, sent.at[0], recv.at[number(3, 0)])
            if j in (0, 1, 2):
                self.send(ref, self.up, sent.at[1], recv.at[number(kind, j + 1)])
            if j in (0, 4, 5, 6):
                self.send(ref, self.down, sent.at[1], recv.at[number(kind, 4 if j == 0 else j + 1)])

        for j in range(8):
            far = j if j <= 3 else j - 3
            for kind in range(4):
                steps.append((far + (0, 1, 1, 2)[kind], lambda kind=kind, j=j: come(kind, j)))
            steps.append((far + 2, lambda j=j: self.sibling(y_of(j), piece, sib)))
        return steps

    def x_first_drain(self, sent):
        wait_bytes(self.weights.at[0, 0:3, 0], sent.at[0])
        wait_bytes(self.weights.at[:, 0:7, 0], sent.at[1])


def steps_at(steps, time):
    return [action for t, action in steps if t == time]


def whole(
    *refs,
):
    operands, loaded = refs[:12], refs[15:27]
    loads = [
        pltpu.make_async_copy(src, dst, refs[-1].at[i]) for i, (src, dst) in enumerate(zip(operands, loaded))
    ]
    for load in loads:
        load.start()
    whole_loaded(loads, *loaded, *refs[12:15], *refs[27:-1])


def whole_loaded(
    loads,
    frames,
    offsets,
    heights,
    widths,
    tokens,
    cotangent,
    space_gain,
    space_qkv,
    space_out,
    time_gain,
    time_qkv,
    time_out,
    out_ref,
    grad_ref,
    gains_ref,
    space_w,
    time_w,
    qkv,
    time_q,
    share,
    time_share,
    hidden_ref,
    hidden_out,
    hidden_in,
    back_out,
    back_in,
    blend_out,
    blend_in,
    front_out,
    front_in,
    sums,
    sums_x,
    sums_y,
    sums_z,
    *sems,
):
    recv, sent, sib_sent, sib_recv, slab_send, slab_recv, slab_own, sum_send, sum_recv = sems
    at = Place()
    rank, plane = at.rank, at.plane
    base = (rank // HALF) * HALF
    me = rank - base

    barrier = pltpu.get_barrier_semaphore()

    def greet(device):
        pl.semaphore_signal(barrier, inc=1, device_id=device, device_id_type=MESH)

    def greet_half(step, carry):
        greet((plane, base + lax.rem(me + step, HALF)))
        return carry

    column = at.x * CORES + at.core

    def on_x(i):
        return at.device(x=i // CORES, core=lax.rem(i, CORES))

    def greet_x(step, carry):
        greet(on_x(lax.rem(column + step, XS * CORES)))
        return carry

    def greet_z(step, carry):
        greet(at.device(plane=lax.rem(plane + step, at.planes)))
        return carry

    lax.fori_loop(1, HALF, greet_half, 0)
    lax.fori_loop(1, XS * CORES, greet_x, 0)
    lax.fori_loop(1, at.planes, greet_z, 0)

    for load in loads:
        load.wait()

    for weights, shard_qkv, shard_out in ((space_w, space_qkv, space_out), (time_w, time_qkv, time_out)):
        own = weights.at[at.x, at.y * CORES + at.core]
        width = shard_qkv.shape[-1]
        own[0] = shard_qkv[0:16, :]
        own[1] = jnp.concatenate(
            [shard_qkv[16:27, :].astype(f32), jnp.zeros((5, width), f32)], axis=0
        ).astype(bf16)
        own[2] = jnp.concatenate([shard_out[...].astype(f32), jnp.zeros((7, width), f32)], axis=0).astype(bf16)

    pl.semaphore_wait(barrier, HALF - 1 + XS * CORES - 1 + at.planes - 1)

    mine = 1 - lax.rem(plane, 2)
    other = 1 - mine

    def streams(gather, i):
        def sib(k):
            return sib_sent.at[k], sib_recv.at[k]

        steps = gather.y_first(
            mine, recv.at[i], sent.at[i], sib(i), other, recv.at[i + 1], sent.at[i + 1], sib(i + 1)
        ) + gather.x_first(2, recv.at[i + 2], sent.at[i + 2], sib(i + 2))

        def drain():
            gather.y_first_drain(sent.at[i], sent.at[i + 1])
            gather.x_first_drain(sent.at[i + 2])
            for k in range(i, i + 3):
                gather.sibling_wait(sib_sent.at[k])

        return steps, drain

    space = Gather(at, space_w)
    space_steps, space_drain = streams(space, 0)
    time_steps, time_drain = streams(Gather(at, time_w), 3)

    def run(steps, time):
        for action in steps_at(steps, time):
            action()

    def arrived(i):
        space.sibling_wait(sib_recv.at[i])

    def slabs_start(i, src, dst):
        def step(i_step, carry):
            k = jnp.where(lax.rem(i_step, 2) == 1, (i_step + 1) // 2, HALF - i_step // 2)
            peer = lax.rem(me + k, HALF)
            pltpu.make_async_remote_copy(
                src_ref=src.at[peer],
                dst_ref=dst.at[me],
                send_sem=slab_send.at[i],
                recv_sem=slab_recv.at[i],
                device_id=(plane, base + peer),
                device_id_type=MESH,
            ).start()
            return carry

        lax.fori_loop(1, HALF, step, 0)
        own = pltpu.make_async_copy(src.at[me], dst.at[me], slab_own.at[i])
        own.start()
        own.wait()

    def slabs_wait(i, dst):
        wait_bytes(dst.at[pl.ds(0, HALF - 1)], slab_recv.at[i])

    def slabs_drain(i, src):
        wait_bytes(src.at[pl.ds(0, HALF - 1)], slab_send.at[i])

    clips = clip_scalars(frames, offsets, heights, widths)
    spread = spread_matrix()

    run(space_steps, 0)
    x = tokens[0].astype(f32)
    _, normed = normed_of(x, gain_row(space_gain))
    for t in range(1, SPACE_DONE):
        run(space_steps, t)
        run(time_steps, t - TIME_AFTER)
    for i in range(3):
        arrived(i)
    run(time_steps, SPACE_DONE - TIME_AFTER)
    count = jnp.int32(0)
    for first, last, size in clips:
        count = count + jnp.where((rank >= first) & (rank < last), size, 0)
    live_space = jnp.where(iota((FRAME, 1), 0) < count, 1.0, 0.0)
    mask_space = iota((FRAME, FRAME), 1) < count
    for g in range(8):
        project(normed, space_w, spread, qkv, g)
        if g == 5:
            run(time_steps, SPACE_DONE - TIME_AFTER + 1)
    blended = []
    for h in range(HEADS):
        s = share_of(qkv[:, head(h)], qkv[:, head(8 + h)], mask_space, 1.0 - live_space)
        share[h] = s
        blended.append((dot_nn(s, qkv[:, head(16 + h)]) * live_space).astype(bf16))
        if h == 3:
            run(time_steps, SPACE_DONE - TIME_AFTER + 2)
    run(time_steps, SPACE_DONE - TIME_AFTER + 3)
    hidden = (x + dot_nn(jnp.concatenate(blended, axis=1), out_rows(space_w))).astype(bf16)
    hidden_ref[...] = hidden
    hidden_out[...] = hidden.reshape(hidden_out.shape)
    slabs_start(0, hidden_out, hidden_in)
    for t in range(SPACE_DONE - TIME_AFTER + 4, 7):
        run(time_steps, t)
    arrived(5)
    back = dot_nt(cotangent[0], out_rows(time_w)).astype(bf16)
    back_out[...] = back.reshape(back_out.shape)
    slabs_start(1, back_out, back_in)
    run(time_steps, 7)

    def tables(shape, dim):
        place = iota(shape, dim)
        tile = base + (place >> 2)
        slot = me * SLOTS + (place & 3)
        ident = jnp.zeros(shape, jnp.int32)
        begin = jnp.zeros(shape, jnp.int32)
        size_of = jnp.zeros(shape, jnp.int32)
        for c, (first, last, size) in enumerate(clips):
            member = (tile >= first) & (tile < last)
            ident = jnp.where(member, c + 1, ident)
            begin = jnp.where(member, first, begin)
            size_of = jnp.where(member, size, size_of)
        time = jnp.where(ident > 0, tile - begin, 0)
        return ident * 4 + (place & 3), time.astype(f32), slot < size_of

    key_q, time, live_q = tables((FRAME, 1), 0)
    key_k, _, live_k = tables((1, FRAME), 1)
    mask = (key_q == key_k) & live_k
    live = jnp.where(live_q, 1.0, 0.0)
    lane = iota((1, LANES), 1)
    pair = ((lane & 63) >> 4) * PIECE + (lane & 15)
    frequency = jnp.exp(pair.astype(f32) * (-math.log(ROPE_BASE) / (HEAD_SIZE // 2)))
    angle = time * frequency
    cosine = jnp.cos(angle)
    sine = jnp.where(lane < 64, -1.0, 1.0) * jnp.sin(angle)

    arrived(3)
    arrived(4)
    slabs_wait(0, hidden_in)
    x_time = hidden_in[...].astype(f32).reshape(FRAME, hidden_in.shape[-1])
    r_time, normed = normed_of(x_time, gain_row(time_gain))
    for g in range(8):
        project(normed, time_w, spread, time_q, g)
    blended = []
    for h in range(HEADS):
        q = time_q[:, head(h)].astype(f32)
        k = time_q[:, head(8 + h)].astype(f32)
        q = (q * cosine + pltpu.roll(q, 64, 1) * sine).astype(bf16)
        k = (k * cosine + pltpu.roll(k, 64, 1) * sine).astype(bf16)
        time_q[:, head(h)] = q
        time_q[:, head(8 + h)] = k
        s = share_of(q, k, mask, 1.0 - live)
        time_share[h] = s
        blended.append((dot_nn(s, time_q[:, head(16 + h)]) * live).astype(bf16))
    blend_out[...] = jnp.concatenate(blended, axis=1).reshape(blend_out.shape)
    slabs_start(2, blend_out, blend_in)
    slabs_wait(1, back_in)
    grads = back_in[...].astype(f32).reshape(FRAME, back_in.shape[-1]) * live
    for h in range(HEADS):
        dq, dk, dv = attend_back(
            time_q[:, head(h)],
            time_q[:, head(8 + h)],
            time_q[:, head(16 + h)],
            time_share[h],
            grads[:, head(h)].astype(bf16),
        )
        dq, dk = dq.astype(f32), dk.astype(f32)
        time_q[:, head(h)] = (dq * cosine - pltpu.roll(dq, 64, 1) * sine).astype(bf16)
        time_q[:, head(8 + h)] = (dk * cosine - pltpu.roll(dk, 64, 1) * sine).astype(bf16)
        time_q[:, head(16 + h)] = dv
    dn = project_back(time_q, time_w, spread).astype(bf16).astype(f32)
    front, d_time_gain = norm_back(x_time, r_time, gain_row(time_gain), dn)
    front_out[...] = front.reshape(front_out.shape)
    slabs_start(3, front_out, front_in)

    slabs_wait(2, blend_in)
    blended = blend_in[...].reshape(FRAME, blend_in.shape[-1])
    out_ref[0] = (hidden_ref[...].astype(f32) + dot_nn(blended, out_rows(time_w))).astype(bf16)

    slabs_wait(3, front_in)
    front = front_in[...].astype(f32).reshape(FRAME, front_in.shape[-1])
    d_hidden = (cotangent[0].astype(f32) + front).astype(bf16)
    d_blended = (dot_nt(d_hidden, out_rows(space_w)).astype(bf16).astype(f32) * live_space).astype(bf16)
    for h in range(HEADS):
        dq, dk, dv = attend_back(
            qkv[:, head(h)], qkv[:, head(8 + h)], qkv[:, head(16 + h)], share[h], d_blended[:, head(h)]
        )
        qkv[:, head(h)] = dq
        qkv[:, head(8 + h)] = dk
        qkv[:, head(16 + h)] = dv
    dn = project_back(qkv, space_w, spread).astype(bf16).astype(f32)
    x = tokens[0].astype(f32)
    r, _ = normed_of(x, gain_row(space_gain))
    dx, d_space_gain = norm_back(x, r, gain_row(space_gain), dn)

    def reduce(i, size, mine, held, to):
        held[mine] = sums[...]

        def step(k, carry):
            pltpu.make_async_remote_copy(
                src_ref=sums,
                dst_ref=held.at[mine],
                send_sem=sum_send.at[i],
                recv_sem=sum_recv.at[i],
                device_id=to(lax.rem(mine + k, size)),
                device_id_type=MESH,
            ).start()
            return carry

        lax.fori_loop(1, size, step, 0)

    def reduced(i, size, held):
        if size > 1:
            wait_bytes(held.at[pl.ds(0, size - 1)], sum_recv.at[i])
            wait_bytes(held.at[pl.ds(0, size - 1)], sum_send.at[i])
        total = held[0]
        for k in range(1, size):
            total = total + held[k]
        return total

    sums[0:1] = d_space_gain
    sums[1:2] = d_time_gain
    reduce(0, XS * CORES, column, sums_x, on_x)
    grad_ref[0] = (d_hidden.astype(f32) + dx.astype(f32)).astype(bf16)
    total = reduced(0, XS * CORES, sums_x)
    sums[...] = total
    reduce(1, YS, at.y, sums_y, lambda i: at.device(y=i))
    for i, src in ((0, hidden_out), (1, back_out), (2, blend_out), (3, front_out)):
        slabs_drain(i, src)
    total = reduced(1, YS, sums_y)
    sums[...] = total
    reduce(2, at.planes, plane, sums_z, lambda i: at.device(plane=i))
    space_drain()
    time_drain()
    total = reduced(2, at.planes, sums_z)
    gains_ref[...] = total * (1.0 / math.sqrt(at.planes * XS * YS * CORES * FRAME))


VMEM_SPEC = pl.BlockSpec(memory_space=pltpu.VMEM)
HBM_SPEC = pl.BlockSpec(memory_space=pltpu.HBM)
LIMIT = 56 * 1024 * 1024


def shards(
    tokens,
    cotangent,
    clip_frames,
    clip_offsets,
    clip_heights,
    clip_widths,
    spatial_gain,
    spatial_qkv,
    spatial_out,
    temporal_gain,
    temporal_qkv,
    temporal_out,
):
    width = tokens.shape[2]
    inner = HEADS * LANES
    planes = lax.axis_size("dp")
    dma = pltpu.SemaphoreType.DMA

    def slab(columns):
        return pltpu.VMEM((HALF, SLOTS, columns), bf16)

    gather_sems = [dma((6, 31)), dma((6, 2)), dma((6,)), dma((6,))]
    operands = (
        clip_frames,
        clip_offsets,
        clip_heights,
        clip_widths,
        tokens,
        cotangent,
        spatial_gain,
        spatial_qkv,
        spatial_out,
        temporal_gain,
        temporal_qkv,
        temporal_out,
    )
    loaded = [pltpu.SMEM(a.shape, a.dtype) for a in operands[:4]]
    loaded += [pltpu.VMEM(a.shape, a.dtype) for a in operands[4:]]
    return pl.pallas_call(
        whole,
        out_shape=[
            jax.ShapeDtypeStruct(tokens.shape, bf16),
            jax.ShapeDtypeStruct(tokens.shape, bf16),
            jax.ShapeDtypeStruct((2, width), f32),
        ],
        in_specs=[HBM_SPEC] * 12,
        out_specs=[VMEM_SPEC] * 3,
        scratch_shapes=loaded
        + [
            pltpu.VMEM((XS, YS * CORES, 3, 16, width), bf16),
            pltpu.VMEM((XS, YS * CORES, 3, 16, width), bf16),
            pltpu.VMEM((FRAME, 3 * inner), bf16),
            pltpu.VMEM((FRAME, 3 * inner), bf16),
            pltpu.VMEM((HEADS, FRAME, FRAME), bf16),
            pltpu.VMEM((HEADS, FRAME, FRAME), bf16),
            pltpu.VMEM((FRAME, width), bf16),
            slab(width),
            slab(width),
            slab(inner),
            slab(inner),
            slab(inner),
            slab(inner),
            slab(width),
            slab(width),
            pltpu.VMEM((2, width), f32),
            pltpu.VMEM((XS * CORES, 2, width), f32),
            pltpu.VMEM((YS, 2, width), f32),
            pltpu.VMEM((planes, 2, width), f32),
        ]
        + gather_sems
        + [dma((4,)), dma((4,)), dma((4,)), dma((3,)), dma((3,)), dma((12,))],
        compiler_params=pltpu.CompilerParams(
            collective_id=0, has_side_effects=True, vmem_limit_bytes=LIMIT
        ),
    )(*operands)


def solution(mesh):
    return jax.shard_map(
        shards,
        mesh=mesh,
        in_specs=(
            P("dp", "ctx", None),
            P("dp", "ctx", None),
            P("dp", None),
            P("dp", None),
            P("dp", None),
            P("dp", None),
            P(),
            P("ctx", None),
            P("ctx", None),
            P(),
            P("ctx", None),
            P("ctx", None),
        ),
        out_specs=(P("dp", "ctx", None), P("dp", "ctx", None), P()),
        check_vma=False,
    )
```

```python
import math

import jax
import jax.numpy as jnp
from jax import lax
from jax.experimental import pallas as pl
from jax.experimental.pallas import tpu as pltpu
from jax.sharding import PartitionSpec as P

HEADS = 8
FRAME = 128
LANES = 128
EPSILON = 1e-06
ROPE_BASE = 10000.0
HEAD_SIZE = 72
PIECE = 9
PIECE_PAD = 16
QKV_PAD = 32
GROUP = 256
GROUP_HEADS = 3 * LANES
HALF = 32
bf16 = jnp.bfloat16
f32 = jnp.float32
MESH = pl.DeviceIdType.MESH


def dot_nn(a, b):
    return lax.dot_general(a, b, (((1,), (0,)), ((), ())), preferred_element_type=f32)


def dot_nt(a, b):
    return lax.dot_general(a, b, (((1,), (1,)), ((), ())), preferred_element_type=f32)


def dot_tn(a, b):
    return lax.dot_general(a, b, (((0,), (0,)), ((), ())), preferred_element_type=f32)


def iota(shape, dim):
    return lax.broadcasted_iota(jnp.int32, shape, dim)


def spread_matrix():
    lane = iota((GROUP, GROUP_HEADS), 1)
    row = iota((GROUP, GROUP_HEADS), 0)
    block = lane >> 4
    within = lane & 15
    third = ((block * 11) >> 5)
    source = third * QKV_PAD + (block - 3 * third) * PIECE + within
    return jnp.where((row == source) & (within < PIECE), 1.0, 0.0).astype(bf16)


def normed_of(x, gain):
    r = lax.rsqrt(jnp.mean(x * x, axis=-1, keepdims=True) + EPSILON)
    return r, (x * r * gain).astype(bf16)


def norm_back(x, r, gain, dn):
    d_gain = jnp.sum(dn * (x * r), axis=0, keepdims=True)
    u = dn * gain
    inner = jnp.sum(u * x, axis=-1, keepdims=True) * (1.0 / x.shape[-1])
    return (r * u - x * (r * r * r * inner)).astype(bf16), d_gain


PIECES = 5
SPACE_QKV, OUT_PIECE, TIME_QKV = 0, 2, 3
LOW, HIGH_AT = 7, 11


def qkv_rows(weights, first, g):
    half = slice(8 * (g % 2), 8 * (g % 2) + 8)
    return weights[g // 2, half, first : first + 2].reshape(GROUP, weights.shape[-1])


def project(normed, weights, first, spread, into, g):
    part = dot_nt(normed, qkv_rows(weights, first, g)).astype(bf16)
    into[:, g * GROUP_HEADS : (g + 1) * GROUP_HEADS] = dot_nn(part, spread).astype(bf16)


def project_back(grads, weights, first, spread):
    parts = [
        dot_nt(grads[:, g * GROUP_HEADS : (g + 1) * GROUP_HEADS], spread).astype(bf16) for g in range(8)
    ]
    rows = weights[:, :, first : first + 2].reshape(8 * GROUP, weights.shape[-1])
    return dot_nn(jnp.concatenate(parts, axis=1), rows)


def piece_rows(weights, piece):
    return weights[:, :, piece].reshape(HEADS * LANES, weights.shape[-1])


def by_head(values, change):
    return jnp.concatenate([change(values[:, head(h)]) for h in range(HEADS)], axis=1)


def time_out_forward(blended, weights):
    within = iota((1, LANES), 1) & 15
    wide = blended.astype(f32)
    low = by_head(wide, lambda v: jnp.where(within >= PIECE, pltpu.roll(v, PIECE, 1), 0.0)).astype(bf16)
    is_high = (within >= HIGH_AT) & (within < HIGH_AT + PIECE - LOW)
    high = by_head(wide, lambda v: jnp.where(is_high, pltpu.roll(v, HIGH_AT - LOW, 1), 0.0)).astype(bf16)
    return dot_nn(low, piece_rows(weights, OUT_PIECE)) + dot_nn(high, piece_rows(weights, TIME_QKV + 1))


def time_out_back(grads, weights):
    within = iota((1, LANES), 1) & 15
    low = by_head(dot_nt(grads, piece_rows(weights, OUT_PIECE)), lambda v: pltpu.roll(v, LANES - PIECE, 1))
    high = by_head(
        dot_nt(grads, piece_rows(weights, TIME_QKV + 1)), lambda v: pltpu.roll(v, LANES - (HIGH_AT - LOW), 1)
    )
    within = jnp.concatenate([within] * HEADS, axis=1)
    return jnp.where(within < LOW, low, jnp.where(within < PIECE, high, 0.0))


SCALE = HEAD_SIZE ** (-0.5)


def shares_of(queries, keys, mask, dead):
    scores = [dot_nt(q, k) for q, k in zip(queries, keys)]
    weights = [jnp.where(mask, jnp.exp(s * SCALE), 0.0) for s in scores]
    totals = [jnp.sum(w, axis=-1, keepdims=True) + dead for w in weights]
    return [(w / t).astype(bf16) for w, t in zip(weights, totals)]


def attend_back(queries, keys, values, shares, grads):
    ds = [dot_nt(g, v).astype(bf16).astype(f32) for g, v in zip(grads, values)]
    dv = [dot_tn(p, g).astype(bf16) for p, g in zip(shares, grads)]
    wide = [p.astype(f32) for p in shares]
    inner = [jnp.sum(d * p, axis=-1, keepdims=True) for d, p in zip(ds, wide)]
    d = [(p * (x - c) * SCALE).astype(bf16) for p, x, c in zip(wide, ds, inner)]
    dq = [dot_nn(x, k).astype(bf16) for x, k in zip(d, keys)]
    dk = [dot_tn(x, q).astype(bf16) for x, q in zip(d, queries)]
    return dq, dk, dv


TOGETHER = 8


def head_groups():
    return [range(h, h + TOGETHER) for h in range(0, HEADS, TOGETHER)]


def head(h):
    return slice(h * LANES, (h + 1) * LANES)


def clip_scalars(frames, offsets, heights, widths):
    out = []
    for c in range(8):
        start = offsets[0, c] >> 7
        out.append((start, start + frames[0, c], heights[0, c] * widths[0, c]))
    return out


XS, YS, CORES = 4, 8, 2
SPACE_DONE, TIME_AFTER = 8, 2
SLOTS = FRAME // HALF


def wait_bytes(ref, sem):
    pltpu.make_async_copy(ref, ref, sem).wait()


def gain_row(gain):
    return gain[...].reshape(1, gain.shape[0])


class Place:
    def __init__(self):
        self.plane = lax.axis_index("dp")
        self.planes = lax.axis_size("dp")
        self.rank = lax.axis_index("ctx")
        self.x = self.rank // (YS * CORES)
        self.y = lax.rem(self.rank // CORES, YS)
        self.core = lax.rem(self.rank, CORES)

    def device(self, x=None, y=None, core=None, plane=None):
        x = self.x if x is None else x
        y = self.y if y is None else y
        core = self.core if core is None else core
        plane = self.plane if plane is None else plane
        return (plane, (x * YS + y) * CORES + core)

    def dx(self, step):
        return lax.rem(self.x + step + XS, XS)

    def dy(self, step):
        return lax.rem(self.y + step + YS, YS)

    def dz(self, step):
        return lax.rem(self.plane + step + self.planes, self.planes)


class Gather:
    def __init__(self, at, weights):
        self.at = at
        self.weights = weights
        self.up, self.down = at.device(y=at.dy(1)), at.device(y=at.dy(-1))
        self.right, self.left = at.device(x=at.dx(1)), at.device(x=at.dx(-1))
        self.above, self.below = at.device(plane=at.dz(1)), at.device(plane=at.dz(-1))

    def block(self, x, y, piece):
        return self.weights.at[x, y * CORES + self.at.core, piece]

    def x_of(self, kind):
        return (self.at.x, self.at.dx(-1), self.at.dx(1), self.at.dx(2))[kind]

    def send(self, ref, device, send_sem, recv_sem):
        pltpu.make_async_remote_copy(
            src_ref=ref, dst_ref=ref, send_sem=send_sem, recv_sem=recv_sem, device_id=device, device_id_type=MESH
        ).start()

    def sibling(self, y, piece, sems):
        at = self.at
        ref = self.weights.at[:, y * CORES + at.core, piece]
        self.send(ref, at.device(core=1 - at.core), sems[0], sems[1])

    def sibling_wait(self, sem):
        wait_bytes(self.weights.at[:, 0:8, 0], sem)

    def y_first(self, piece, recv, sent, sib, other=None, z_recv=None, z_sent=None, z_sib=None):
        at = self.at
        steps = []

        def y_of(j):
            return at.dy(-j) if j <= 4 else at.dy(j - 4)

        def ident(kind, j):
            return j - 1 if kind == 0 else 7 + (kind - 1) * 8 + j

        def over_z(kind, j):
            if other is not None:
                i = ident(kind, j)
                ref = self.block(self.x_of(kind), y_of(j), piece)
                self.send(ref, self.above if i % 2 == 0 else self.below, z_sent.at[i % 2], z_recv.at[i])

        def along_y(j, what, sems, come):
            ref = self.block(at.x, y_of(j), what)
            if j > 0:
                wait_bytes(ref, come.at[ident(0, j)])
            if j in (0, 1, 2, 3):
                self.send(ref, self.up, sems, come.at[ident(0, j + 1)])
            if j in (0, 5, 6):
                self.send(ref, self.down, sems, come.at[ident(0, 5 if j == 0 else j + 1)])

        plus = (0, 1, 2, 3)

        def arrive_y(j):
            along_y(j, piece, sent.at[0], recv)
            ref = self.block(at.x, y_of(j), piece)
            self.send(ref, self.right, sent.at[1], recv.at[ident(1, j)])
            self.send(ref, self.left, sent.at[1], recv.at[ident(2, j)])
            if other is not None:
                along_y(j, other, z_sent.at[2], z_recv)

        def arrive_x(kind, j):
            ref = self.block(self.x_of(kind), y_of(j), piece)
            wait_bytes(ref, recv.at[ident(kind, j)])
            if kind == 1 and j in plus:
                self.send(ref, self.right, sent.at[1], recv.at[ident(3, j)])
            if kind == 2 and j not in plus:
                self.send(ref, self.left, sent.at[1], recv.at[ident(3, j)])
            over_z(kind, j)

        def arrive_z(j):
            for kind in (1, 2, 3):
                wait_bytes(self.block(self.x_of(kind), y_of(j), other), z_recv.at[ident(kind, j)])
            self.sibling(y_of(j), other, z_sib)

        for j in range(8):
            far = j if j <= 4 else j - 4
            steps.append((far, lambda j=j: arrive_y(j)))
            for kind in (1, 2, 3):
                steps.append((far + (1 if kind < 3 else 2), lambda kind=kind, j=j: arrive_x(kind, j)))
            steps.append((far + 2, lambda j=j: self.sibling(y_of(j), piece, sib)))
            if other is not None:
                steps.append((far + 3, lambda j=j: arrive_z(j)))
        return steps

    def y_first_drain(self, sent, z_sent=None):
        wait_bytes(self.weights.at[0, 0:7, 0], sent.at[0])
        wait_bytes(self.weights.at[0:3, 0:8, 0], sent.at[1])
        if z_sent is not None:
            wait_bytes(self.weights.at[0, 0:12, 0], z_sent.at[0])
            wait_bytes(self.weights.at[0, 0:12, 0], z_sent.at[1])
            wait_bytes(self.weights.at[0, 0:7, 0], z_sent.at[2])

    def x_first(self, piece, recv, sent, sib):
        at = self.at
        steps = []

        def y_of(j):
            return at.dy(-j) if j <= 3 else at.dy(j - 3)

        def number(kind, j):
            return kind - 1 if j == 0 else 3 + kind * 7 + j - 1

        def come(kind, j):
            ref = self.block(self.x_of(kind), y_of(j), piece)
            if kind > 0 or j > 0:
                wait_bytes(ref, recv.at[number(kind, j)])
            if j == 0 and kind == 0:
                self.send(ref, self.right, sent.at[0], recv.at[number(1, 0)])
                self.send(ref, self.left, sent.at[0], recv.at[number(2, 0)])
            if j == 0 and kind == 2:
                self.send(ref, self.left, sent.at[0], recv.at[number(3, 0)])
            if j in (0, 1, 2):
                self.send(ref, self.up, sent.at[1], recv.at[number(kind, j + 1)])
            if j in (0, 4, 5, 6):
                self.send(ref, self.down, sent.at[1], recv.at[number(kind, 4 if j == 0 else j + 1)])

        for j in range(8):
            far = j if j <= 3 else j - 3
            for kind in range(4):
                steps.append((far + (0, 1, 1, 2)[kind], lambda kind=kind, j=j: come(kind, j)))
            steps.append((far + 2, lambda j=j: self.sibling(y_of(j), piece, sib)))
        return steps

    def x_first_drain(self, sent):
        wait_bytes(self.weights.at[0, 0:3, 0], sent.at[0])
        wait_bytes(self.weights.at[:, 0:7, 0], sent.at[1])


def steps_at(steps, time):
    return [action for t, action in steps if t == time]


def whole(
    *refs,
):
    operands, loaded = refs[:12], refs[15:27]
    loads = [
        pltpu.make_async_copy(src, dst, refs[-1].at[i]) for i, (src, dst) in enumerate(zip(operands, loaded))
    ]
    for load in loads:
        load.start()
    whole_loaded(loads, *loaded, *refs[12:15], *refs[27:-1])


def whole_loaded(
    loads,
    frames,
    offsets,
    heights,
    widths,
    tokens,
    cotangent,
    space_gain,
    space_qkv,
    space_out,
    time_gain,
    time_qkv,
    time_out,
    out_ref,
    grad_ref,
    gains_ref,
    weights,
    qkv,
    time_q,
    share,
    time_share,
    hidden_ref,
    hidden_out,
    hidden_in,
    back_out,
    back_in,
    blend_out,
    blend_in,
    front_out,
    front_in,
    sums,
    sums_x,
    sums_y,
    sums_z,
    *sems,
):
    recv, sent, sib_sent, sib_recv, slab_send, slab_recv, slab_own, sum_send, sum_recv = sems
    at = Place()
    rank, plane = at.rank, at.plane
    base = (rank // HALF) * HALF
    me = rank - base

    barrier = pltpu.get_barrier_semaphore()

    def greet(device):
        pl.semaphore_signal(barrier, inc=1, device_id=device, device_id_type=MESH)

    def greet_half(step, carry):
        greet((plane, base + lax.rem(me + step, HALF)))
        return carry

    column = at.x * CORES + at.core

    def on_x(i):
        return at.device(x=i // CORES, core=lax.rem(i, CORES))

    def greet_x(step, carry):
        greet(on_x(lax.rem(column + step, XS * CORES)))
        return carry

    def greet_z(step, carry):
        greet(at.device(plane=lax.rem(plane + step, at.planes)))
        return carry

    lax.fori_loop(1, HALF, greet_half, 0)
    lax.fori_loop(1, XS * CORES, greet_x, 0)
    lax.fori_loop(1, at.planes, greet_z, 0)

    for load in loads:
        load.wait()

    own = weights.at[at.x, at.y * CORES + at.core]
    width = space_qkv.shape[-1]

    def padded(*parts):
        rows = sum(p.shape[0] for p in parts)
        parts = [p.astype(f32) for p in parts] + [jnp.zeros((16 - rows, width), f32)] * (rows < 16)
        return jnp.concatenate(parts, axis=0).astype(bf16)

    own[SPACE_QKV] = space_qkv[0:16, :]
    own[SPACE_QKV + 1] = padded(space_qkv[16:27, :])
    own[OUT_PIECE] = padded(space_out[...], time_out[0:LOW, :])
    own[TIME_QKV] = time_qkv[0:16, :]
    own[TIME_QKV + 1] = padded(time_qkv[16:27, :], time_out[LOW:PIECE, :])

    pl.semaphore_wait(barrier, HALF - 1 + XS * CORES - 1 + at.planes - 1)

    mine = 1 - lax.rem(plane, 2)
    other = 1 - mine
    gather = Gather(at, weights)

    def sib(k):
        return sib_sent.at[k], sib_recv.at[k]

    def pair(first, i):
        return gather.y_first(
            first + mine, recv.at[i], sent.at[i], sib(i), first + other, recv.at[i + 1], sent.at[i + 1], sib(i + 1)
        )

    space_steps = pair(SPACE_QKV, 0) + gather.x_first(OUT_PIECE, recv.at[2], sent.at[2], sib(2))
    time_steps = pair(TIME_QKV, 3)
    time_left = list(range(SPACE_DONE - TIME_AFTER, SPACE_DONE))

    def drain():
        gather.y_first_drain(sent.at[0], sent.at[1])
        gather.x_first_drain(sent.at[2])
        gather.y_first_drain(sent.at[3], sent.at[4])
        for k in range(PIECES):
            gather.sibling_wait(sib_sent.at[k])

    def run(steps, time):
        for action in steps_at(steps, time):
            action()

    def run_next():
        if time_left:
            run(time_steps, time_left.pop(0))

    def arrived(i):
        gather.sibling_wait(sib_recv.at[i])

    def slabs_start(i, src, dst):
        def step(i_step, carry):
            k = jnp.where(lax.rem(i_step, 2) == 1, (i_step + 1) // 2, HALF - i_step // 2)
            peer = lax.rem(me + k, HALF)
            pltpu.make_async_remote_copy(
                src_ref=src.at[peer],
                dst_ref=dst.at[me],
                send_sem=slab_send.at[i],
                recv_sem=slab_recv.at[i],
                device_id=(plane, base + peer),
                device_id_type=MESH,
            ).start()
            return carry

        lax.fori_loop(1, HALF, step, 0)
        own = pltpu.make_async_copy(src.at[me], dst.at[me], slab_own.at[i])
        own.start()
        own.wait()

    def slabs_wait(i, dst):
        wait_bytes(dst.at[pl.ds(0, HALF - 1)], slab_recv.at[i])

    def slabs_drain(i, src):
        wait_bytes(src.at[pl.ds(0, HALF - 1)], slab_send.at[i])

    clips = clip_scalars(frames, offsets, heights, widths)
    spread = spread_matrix()

    run(space_steps, 0)
    x = tokens[0].astype(f32)
    _, normed = normed_of(x, gain_row(space_gain))
    for t in range(1, SPACE_DONE):
        run(space_steps, t)
        run(time_steps, t - TIME_AFTER)
    for i in range(3):
        arrived(i)
    count = jnp.int32(0)
    for first, last, size in clips:
        count = count + jnp.where((rank >= first) & (rank < last), size, 0)
    live_space = jnp.where(iota((FRAME, 1), 0) < count, 1.0, 0.0)
    mask_space = iota((FRAME, FRAME), 1) < count
    for g in range(8):
        project(normed, weights, SPACE_QKV, spread, qkv, g)
        if g in (3, 7):
            run_next()
    blended = []
    for heads in head_groups():
        shares = shares_of(
            [qkv[:, head(h)] for h in heads], [qkv[:, head(8 + h)] for h in heads], mask_space, 1.0 - live_space
        )
        mixed = [dot_nn(p, qkv[:, head(16 + h)]) for p, h in zip(shares, heads)]
        for h, p, m in zip(heads, shares, mixed):
            share[h] = p
            blended.append((m * live_space).astype(bf16))
    run_next()
    hidden = (x + dot_nn(jnp.concatenate(blended, axis=1), piece_rows(weights, OUT_PIECE))).astype(bf16)
    hidden_ref[...] = hidden
    hidden_out[...] = hidden.reshape(hidden_out.shape)
    slabs_start(0, hidden_out, hidden_in)
    while time_left:
        run_next()
    arrived(3)
    arrived(4)
    back = time_out_back(cotangent[0], weights).astype(bf16)
    back_out[...] = back.reshape(back_out.shape)
    slabs_start(1, back_out, back_in)

    def tables(shape, dim):
        place = iota(shape, dim)
        tile = base + (place >> 2)
        slot = me * SLOTS + (place & 3)
        ident = jnp.zeros(shape, jnp.int32)
        begin = jnp.zeros(shape, jnp.int32)
        size_of = jnp.zeros(shape, jnp.int32)
        for c, (first, last, size) in enumerate(clips):
            member = (tile >= first) & (tile < last)
            ident = jnp.where(member, c + 1, ident)
            begin = jnp.where(member, first, begin)
            size_of = jnp.where(member, size, size_of)
        time = jnp.where(ident > 0, tile - begin, 0)
        return ident * 4 + (place & 3), time.astype(f32), slot < size_of

    key_q, time, live_q = tables((FRAME, 1), 0)
    key_k, _, live_k = tables((1, FRAME), 1)
    mask = (key_q == key_k) & live_k
    live = jnp.where(live_q, 1.0, 0.0)
    lane = iota((1, LANES), 1)
    pair = ((lane & 63) >> 4) * PIECE + (lane & 15)
    frequency = jnp.exp(pair.astype(f32) * (-math.log(ROPE_BASE) / (HEAD_SIZE // 2)))
    angle = time * frequency
    cosine = jnp.cos(angle)
    sine = jnp.where(lane < 64, -1.0, 1.0) * jnp.sin(angle)

    slabs_wait(0, hidden_in)
    x_time = hidden_in[...].astype(f32).reshape(FRAME, hidden_in.shape[-1])
    r_time, normed = normed_of(x_time, gain_row(time_gain))
    for g in range(8):
        project(normed, weights, TIME_QKV, spread, time_q, g)
    def turned(v):
        v = v.astype(f32)
        return (v * cosine + pltpu.roll(v, 64, 1) * sine).astype(bf16)

    def turned_back(v):
        v = v.astype(f32)
        return (v * cosine - pltpu.roll(v, 64, 1) * sine).astype(bf16)

    blended = []
    for heads in head_groups():
        queries = [turned(time_q[:, head(h)]) for h in heads]
        keys = [turned(time_q[:, head(8 + h)]) for h in heads]
        shares = shares_of(queries, keys, mask, 1.0 - live)
        mixed = [dot_nn(p, time_q[:, head(16 + h)]) for p, h in zip(shares, heads)]
        for h, q, k, p, m in zip(heads, queries, keys, shares, mixed):
            time_q[:, head(h)] = q
            time_q[:, head(8 + h)] = k
            time_share[h] = p
            blended.append((m * live).astype(bf16))
    blend_out[...] = jnp.concatenate(blended, axis=1).reshape(blend_out.shape)
    slabs_start(2, blend_out, blend_in)
    slabs_wait(1, back_in)
    grads = back_in[...].astype(f32).reshape(FRAME, back_in.shape[-1]) * live
    for heads in head_groups():
        dq, dk, dv = attend_back(
            [time_q[:, head(h)] for h in heads],
            [time_q[:, head(8 + h)] for h in heads],
            [time_q[:, head(16 + h)] for h in heads],
            [time_share[h] for h in heads],
            [grads[:, head(h)].astype(bf16) for h in heads],
        )
        dq, dk = [turned_back(v) for v in dq], [turned_back(v) for v in dk]
        for i, h in enumerate(heads):
            time_q[:, head(h)] = dq[i]
            time_q[:, head(8 + h)] = dk[i]
            time_q[:, head(16 + h)] = dv[i]
    dn = project_back(time_q, weights, TIME_QKV, spread).astype(bf16).astype(f32)
    front, d_time_gain = norm_back(x_time, r_time, gain_row(time_gain), dn)
    front_out[...] = front.reshape(front_out.shape)
    slabs_start(3, front_out, front_in)

    slabs_wait(2, blend_in)
    blended = blend_in[...].reshape(FRAME, blend_in.shape[-1])
    out_ref[0] = (hidden_ref[...].astype(f32) + time_out_forward(blended, weights)).astype(bf16)

    slabs_wait(3, front_in)
    front = front_in[...].astype(f32).reshape(FRAME, front_in.shape[-1])
    d_hidden = (cotangent[0].astype(f32) + front).astype(bf16)
    d_blended = (dot_nt(d_hidden, piece_rows(weights, OUT_PIECE)).astype(bf16).astype(f32) * live_space).astype(bf16)
    for heads in head_groups():
        dq, dk, dv = attend_back(
            [qkv[:, head(h)] for h in heads],
            [qkv[:, head(8 + h)] for h in heads],
            [qkv[:, head(16 + h)] for h in heads],
            [share[h] for h in heads],
            [d_blended[:, head(h)] for h in heads],
        )
        for i, h in enumerate(heads):
            qkv[:, head(h)] = dq[i]
            qkv[:, head(8 + h)] = dk[i]
            qkv[:, head(16 + h)] = dv[i]
    dn = project_back(qkv, weights, SPACE_QKV, spread).astype(bf16).astype(f32)
    x = tokens[0].astype(f32)
    r, _ = normed_of(x, gain_row(space_gain))
    dx, d_space_gain = norm_back(x, r, gain_row(space_gain), dn)

    def reduce(i, size, mine, held, to):
        held[mine] = sums[...]

        def step(k, carry):
            pltpu.make_async_remote_copy(
                src_ref=sums,
                dst_ref=held.at[mine],
                send_sem=sum_send.at[i],
                recv_sem=sum_recv.at[i],
                device_id=to(lax.rem(mine + k, size)),
                device_id_type=MESH,
            ).start()
            return carry

        lax.fori_loop(1, size, step, 0)

    def reduced(i, size, held):
        if size > 1:
            wait_bytes(held.at[pl.ds(0, size - 1)], sum_recv.at[i])
            wait_bytes(held.at[pl.ds(0, size - 1)], sum_send.at[i])
        total = held[0]
        for k in range(1, size):
            total = total + held[k]
        return total

    sums[0:1] = d_space_gain
    sums[1:2] = d_time_gain
    reduce(0, XS * CORES, column, sums_x, on_x)
    grad_ref[0] = (d_hidden.astype(f32) + dx.astype(f32)).astype(bf16)
    total = reduced(0, XS * CORES, sums_x)
    sums[...] = total
    reduce(1, YS, at.y, sums_y, lambda i: at.device(y=i))
    for i, src in ((0, hidden_out), (1, back_out), (2, blend_out), (3, front_out)):
        slabs_drain(i, src)
    total = reduced(1, YS, sums_y)
    sums[...] = total
    reduce(2, at.planes, plane, sums_z, lambda i: at.device(plane=i))
    drain()
    total = reduced(2, at.planes, sums_z)
    gains_ref[...] = total * (1.0 / math.sqrt(at.planes * XS * YS * CORES * FRAME))


VMEM_SPEC = pl.BlockSpec(memory_space=pltpu.VMEM)
HBM_SPEC = pl.BlockSpec(memory_space=pltpu.HBM)
LIMIT = 56 * 1024 * 1024


def shards(
    tokens,
    cotangent,
    clip_frames,
    clip_offsets,
    clip_heights,
    clip_widths,
    spatial_gain,
    spatial_qkv,
    spatial_out,
    temporal_gain,
    temporal_qkv,
    temporal_out,
):
    width = tokens.shape[2]
    inner = HEADS * LANES
    planes = lax.axis_size("dp")
    dma = pltpu.SemaphoreType.DMA

    def slab(columns):
        return pltpu.VMEM((HALF, SLOTS, columns), bf16)

    gather_sems = [dma((PIECES, 31)), dma((PIECES, 3)), dma((PIECES,)), dma((PIECES,))]
    operands = (
        clip_frames,
        clip_offsets,
        clip_heights,
        clip_widths,
        tokens,
        cotangent,
        spatial_gain,
        spatial_qkv,
        spatial_out,
        temporal_gain,
        temporal_qkv,
        temporal_out,
    )
    loaded = [pltpu.SMEM(a.shape, a.dtype) for a in operands[:4]]
    loaded += [pltpu.VMEM(a.shape, a.dtype) for a in operands[4:]]
    return pl.pallas_call(
        whole,
        out_shape=[
            jax.ShapeDtypeStruct(tokens.shape, bf16),
            jax.ShapeDtypeStruct(tokens.shape, bf16),
            jax.ShapeDtypeStruct((2, width), f32),
        ],
        in_specs=[HBM_SPEC] * 12,
        out_specs=[VMEM_SPEC] * 3,
        scratch_shapes=loaded
        + [
            pltpu.VMEM((XS, YS * CORES, PIECES, 16, width), bf16),
            pltpu.VMEM((FRAME, 3 * inner), bf16),
            pltpu.VMEM((FRAME, 3 * inner), bf16),
            pltpu.VMEM((HEADS, FRAME, FRAME), bf16),
            pltpu.VMEM((HEADS, FRAME, FRAME), bf16),
            pltpu.VMEM((FRAME, width), bf16),
            slab(width),
            slab(width),
            slab(inner),
            slab(inner),
            slab(inner),
            slab(inner),
            slab(width),
            slab(width),
            pltpu.VMEM((2, width), f32),
            pltpu.VMEM((XS * CORES, 2, width), f32),
            pltpu.VMEM((YS, 2, width), f32),
            pltpu.VMEM((planes, 2, width), f32),
        ]
        + gather_sems
        + [dma((4,)), dma((4,)), dma((4,)), dma((3,)), dma((3,)), dma((12,))],
        compiler_params=pltpu.CompilerParams(
            collective_id=0, has_side_effects=True, vmem_limit_bytes=LIMIT
        ),
    )(*operands)


def solution(mesh):
    return jax.shard_map(
        shards,
        mesh=mesh,
        in_specs=(
            P("dp", "ctx", None),
            P("dp", "ctx", None),
            P("dp", None),
            P("dp", None),
            P("dp", None),
            P("dp", None),
            P(),
            P("ctx", None),
            P("ctx", None),
            P(),
            P("ctx", None),
            P("ctx", None),
        ),
        out_specs=(P("dp", "ctx", None), P("dp", "ctx", None), P()),
        check_vma=False,
    )
```

```python
import math

import jax
import jax.numpy as jnp
from jax import lax
from jax.experimental import pallas as pl
from jax.experimental.pallas import tpu as pltpu
from jax.sharding import PartitionSpec as P

HEADS = 8
FRAME = 128
LANES = 128
EPSILON = 1e-06
ROPE_BASE = 10000.0
HEAD_SIZE = 72
PIECE = 9
PIECE_PAD = 16
QKV_PAD = 32
GROUP = 256
GROUP_HEADS = 3 * LANES
HALF = 32
bf16 = jnp.bfloat16
f32 = jnp.float32
MESH = pl.DeviceIdType.MESH


def dot_nn(a, b):
    return lax.dot_general(a, b, (((1,), (0,)), ((), ())), preferred_element_type=f32)


def dot_nt(a, b):
    return lax.dot_general(a, b, (((1,), (1,)), ((), ())), preferred_element_type=f32)


def dot_tn(a, b):
    return lax.dot_general(a, b, (((0,), (0,)), ((), ())), preferred_element_type=f32)


def iota(shape, dim):
    return lax.broadcasted_iota(jnp.int32, shape, dim)


def spread_matrix():
    lane = iota((GROUP, GROUP_HEADS), 1)
    row = iota((GROUP, GROUP_HEADS), 0)
    block = lane >> 4
    within = lane & 15
    third = ((block * 11) >> 5)
    source = third * QKV_PAD + (block - 3 * third) * PIECE + within
    return jnp.where((row == source) & (within < PIECE), 1.0, 0.0).astype(bf16)


def normed_of(x, gain):
    r = lax.rsqrt(jnp.mean(x * x, axis=-1, keepdims=True) + EPSILON)
    return r, (x * r * gain).astype(bf16)


def norm_back(x, r, gain, dn):
    d_gain = jnp.sum(dn * (x * r), axis=0, keepdims=True)
    u = dn * gain
    inner = jnp.sum(u * x, axis=-1, keepdims=True) * (1.0 / x.shape[-1])
    return (r * u - x * (r * r * r * inner)).astype(bf16), d_gain


PIECES = 5
SPACE_QKV, OUT_PIECE, TIME_QKV = 0, 2, 3
LOW, HIGH_AT = 7, 11


def qkv_rows(weights, first, g):
    half = slice(8 * (g % 2), 8 * (g % 2) + 8)
    return weights[g // 2, half, first : first + 2].reshape(GROUP, weights.shape[-1])


def project(normed, weights, first, spread, into, g):
    part = dot_nt(normed, qkv_rows(weights, first, g)).astype(bf16)
    into[:, g * GROUP_HEADS : (g + 1) * GROUP_HEADS] = dot_nn(part, spread).astype(bf16)


def project_back(grads, weights, first, spread):
    parts = [
        dot_nt(grads[:, g * GROUP_HEADS : (g + 1) * GROUP_HEADS], spread).astype(bf16) for g in range(8)
    ]
    rows = weights[:, :, first : first + 2].reshape(8 * GROUP, weights.shape[-1])
    return dot_nn(jnp.concatenate(parts, axis=1), rows)


def piece_rows(weights, piece):
    return weights[:, :, piece].reshape(HEADS * LANES, weights.shape[-1])


def by_head(values, change):
    return jnp.concatenate([change(values[:, head(h)]) for h in range(HEADS)], axis=1)


def time_out_forward(blended, weights):
    within = iota((1, LANES), 1) & 15
    wide = blended.astype(f32)
    low = by_head(wide, lambda v: jnp.where(within >= PIECE, pltpu.roll(v, PIECE, 1), 0.0)).astype(bf16)
    is_high = (within >= HIGH_AT) & (within < HIGH_AT + PIECE - LOW)
    high = by_head(wide, lambda v: jnp.where(is_high, pltpu.roll(v, HIGH_AT - LOW, 1), 0.0)).astype(bf16)
    return dot_nn(low, piece_rows(weights, OUT_PIECE)) + dot_nn(high, piece_rows(weights, TIME_QKV + 1))


def time_out_back(grads, weights):
    within = iota((1, LANES), 1) & 15
    low = by_head(dot_nt(grads, piece_rows(weights, OUT_PIECE)), lambda v: pltpu.roll(v, LANES - PIECE, 1))
    high = by_head(
        dot_nt(grads, piece_rows(weights, TIME_QKV + 1)), lambda v: pltpu.roll(v, LANES - (HIGH_AT - LOW), 1)
    )
    within = jnp.concatenate([within] * HEADS, axis=1)
    return jnp.where(within < LOW, low, jnp.where(within < PIECE, high, 0.0))


SCALE = HEAD_SIZE ** (-0.5)


def shares_of(queries, keys, mask, dead):
    scores = [dot_nt(q, k) for q, k in zip(queries, keys)]
    weights = [jnp.where(mask, jnp.exp(s * SCALE), 0.0) for s in scores]
    totals = [jnp.sum(w, axis=-1, keepdims=True) + dead for w in weights]
    return [(w / t).astype(bf16) for w, t in zip(weights, totals)]


def attend_back(queries, keys, values, shares, grads):
    ds = [dot_nt(g, v).astype(bf16).astype(f32) for g, v in zip(grads, values)]
    dv = [dot_tn(p, g).astype(bf16) for p, g in zip(shares, grads)]
    wide = [p.astype(f32) for p in shares]
    inner = [jnp.sum(d * p, axis=-1, keepdims=True) for d, p in zip(ds, wide)]
    d = [(p * (x - c) * SCALE).astype(bf16) for p, x, c in zip(wide, ds, inner)]
    dq = [dot_nn(x, k).astype(bf16) for x, k in zip(d, keys)]
    dk = [dot_tn(x, q).astype(bf16) for x, q in zip(d, queries)]
    return dq, dk, dv


TOGETHER = 8


def head_groups():
    return [range(h, h + TOGETHER) for h in range(0, HEADS, TOGETHER)]


def head(h):
    return slice(h * LANES, (h + 1) * LANES)


def clip_scalars(frames, offsets, heights, widths):
    out = []
    for c in range(8):
        start = offsets[0, c] >> 7
        out.append((start, start + frames[0, c], heights[0, c] * widths[0, c]))
    return out


XS, YS, CORES = 4, 8, 2
SPACE_DONE, TIME_AFTER = 8, 2
SLOTS = FRAME // HALF


def wait_bytes(ref, sem):
    pltpu.make_async_copy(ref, ref, sem).wait()


def gain_row(gain):
    return gain[...].reshape(1, gain.shape[0])


class Place:
    def __init__(self):
        self.plane = lax.axis_index("dp")
        self.planes = lax.axis_size("dp")
        self.rank = lax.axis_index("ctx")
        self.x = self.rank // (YS * CORES)
        self.y = lax.rem(self.rank // CORES, YS)
        self.core = lax.rem(self.rank, CORES)

    def device(self, x=None, y=None, core=None, plane=None):
        x = self.x if x is None else x
        y = self.y if y is None else y
        core = self.core if core is None else core
        plane = self.plane if plane is None else plane
        return (plane, (x * YS + y) * CORES + core)

    def dx(self, step):
        return lax.rem(self.x + step + XS, XS)

    def dy(self, step):
        return lax.rem(self.y + step + YS, YS)

    def dz(self, step):
        return lax.rem(self.plane + step + self.planes, self.planes)


class Gather:
    def __init__(self, at, weights):
        self.at = at
        self.weights = weights
        self.up, self.down = at.device(y=at.dy(1)), at.device(y=at.dy(-1))
        self.right, self.left = at.device(x=at.dx(1)), at.device(x=at.dx(-1))
        self.above, self.below = at.device(plane=at.dz(1)), at.device(plane=at.dz(-1))

    def block(self, x, y, piece):
        return self.weights.at[x, y * CORES + self.at.core, piece]

    def x_of(self, kind):
        return (self.at.x, self.at.dx(-1), self.at.dx(1), self.at.dx(2))[kind]

    def send(self, ref, device, send_sem, recv_sem):
        pltpu.make_async_remote_copy(
            src_ref=ref, dst_ref=ref, send_sem=send_sem, recv_sem=recv_sem, device_id=device, device_id_type=MESH
        ).start()

    def sibling(self, y, piece, sems):
        at = self.at
        ref = self.weights.at[:, y * CORES + at.core, piece]
        self.send(ref, at.device(core=1 - at.core), sems[0], sems[1])

    def sibling_wait(self, sem):
        wait_bytes(self.weights.at[:, 0:8, 0], sem)

    def y_first(self, piece, recv, sent, sib, other=None, z_recv=None, z_sent=None, z_sib=None):
        at = self.at
        steps = []

        def y_of(j):
            return at.dy(-j) if j <= 4 else at.dy(j - 4)

        def ident(kind, j):
            return j - 1 if kind == 0 else 7 + (kind - 1) * 8 + j

        def over_z(kind, j):
            if other is not None:
                i = ident(kind, j)
                ref = self.block(self.x_of(kind), y_of(j), piece)
                self.send(ref, self.above if i % 2 == 0 else self.below, z_sent.at[i % 2], z_recv.at[i])

        def along_y(j, what, sems, come):
            ref = self.block(at.x, y_of(j), what)
            if j > 0:
                wait_bytes(ref, come.at[ident(0, j)])
            if j in (0, 1, 2, 3):
                self.send(ref, self.up, sems, come.at[ident(0, j + 1)])
            if j in (0, 5, 6):
                self.send(ref, self.down, sems, come.at[ident(0, 5 if j == 0 else j + 1)])

        plus = (0, 1, 2, 3)

        def arrive_y(j):
            along_y(j, piece, sent.at[0], recv)
            ref = self.block(at.x, y_of(j), piece)
            self.send(ref, self.right, sent.at[1], recv.at[ident(1, j)])
            self.send(ref, self.left, sent.at[1], recv.at[ident(2, j)])
            if other is not None:
                along_y(j, other, z_sent.at[2], z_recv)

        def arrive_x(kind, j):
            ref = self.block(self.x_of(kind), y_of(j), piece)
            wait_bytes(ref, recv.at[ident(kind, j)])
            if kind == 1 and j in plus:
                self.send(ref, self.right, sent.at[1], recv.at[ident(3, j)])
            if kind == 2 and j not in plus:
                self.send(ref, self.left, sent.at[1], recv.at[ident(3, j)])
            over_z(kind, j)

        def arrive_z(j):
            for kind in (1, 2, 3):
                wait_bytes(self.block(self.x_of(kind), y_of(j), other), z_recv.at[ident(kind, j)])
            self.sibling(y_of(j), other, z_sib)

        for j in range(8):
            far = j if j <= 4 else j - 4
            steps.append((far, 0, lambda j=j: arrive_y(j)))
            for kind in (1, 2, 3):
                steps.append((far + (1 if kind < 3 else 2), 1, lambda kind=kind, j=j: arrive_x(kind, j)))
            steps.append((far + 2, 3, lambda j=j: self.sibling(y_of(j), piece, sib)))
            if other is not None:
                steps.append((far + 3, 2, lambda j=j: arrive_z(j)))
        return steps

    def y_first_drain(self, sent, z_sent=None):
        wait_bytes(self.weights.at[0, 0:7, 0], sent.at[0])
        wait_bytes(self.weights.at[0:3, 0:8, 0], sent.at[1])
        if z_sent is not None:
            wait_bytes(self.weights.at[0, 0:12, 0], z_sent.at[0])
            wait_bytes(self.weights.at[0, 0:12, 0], z_sent.at[1])
            wait_bytes(self.weights.at[0, 0:7, 0], z_sent.at[2])

    def x_first(self, piece, recv, sent, sib):
        at = self.at
        steps = []

        def y_of(j):
            return at.dy(-j) if j <= 3 else at.dy(j - 3)

        def number(kind, j):
            return kind - 1 if j == 0 else 3 + kind * 7 + j - 1

        def come(kind, j):
            ref = self.block(self.x_of(kind), y_of(j), piece)
            if kind > 0 or j > 0:
                wait_bytes(ref, recv.at[number(kind, j)])
            if j == 0 and kind == 0:
                self.send(ref, self.right, sent.at[0], recv.at[number(1, 0)])
                self.send(ref, self.left, sent.at[0], recv.at[number(2, 0)])
            if j == 0 and kind == 2:
                self.send(ref, self.left, sent.at[0], recv.at[number(3, 0)])
            if j in (0, 1, 2):
                self.send(ref, self.up, sent.at[1], recv.at[number(kind, j + 1)])
            if j in (0, 4, 5, 6):
                self.send(ref, self.down, sent.at[1], recv.at[number(kind, 4 if j == 0 else j + 1)])

        for j in range(8):
            far = j if j <= 3 else j - 3
            for kind in range(4):
                steps.append((far + (0, 1, 1, 2)[kind], 1.5, lambda kind=kind, j=j: come(kind, j)))
            steps.append((far + 2, 3, lambda j=j: self.sibling(y_of(j), piece, sib)))
        return steps

    def x_first_drain(self, sent):
        wait_bytes(self.weights.at[0, 0:3, 0], sent.at[0])
        wait_bytes(self.weights.at[:, 0:7, 0], sent.at[1])


def steps_at(steps, time):
    return [action for t, _, action in sorted(steps, key=lambda step: step[1]) if t == time]


def whole(
    *refs,
):
    operands, loaded = refs[:12], refs[15:27]
    loads = [
        pltpu.make_async_copy(src, dst, refs[-1].at[i]) for i, (src, dst) in enumerate(zip(operands, loaded))
    ]
    for load in loads:
        load.start()
    whole_loaded(loads, *loaded, *refs[12:15], *refs[27:-1])


def whole_loaded(
    loads,
    frames,
    offsets,
    heights,
    widths,
    tokens,
    cotangent,
    space_gain,
    space_qkv,
    space_out,
    time_gain,
    time_qkv,
    time_out,
    out_ref,
    grad_ref,
    gains_ref,
    weights,
    qkv,
    time_q,
    share,
    time_share,
    hidden_ref,
    hidden_out,
    hidden_in,
    back_out,
    back_in,
    blend_out,
    blend_in,
    front_out,
    front_in,
    sums,
    sums_x,
    sums_y,
    sums_z,
    *sems,
):
    recv, sent, sib_sent, sib_recv, slab_send, slab_recv, slab_own, sum_send, sum_recv = sems
    at = Place()
    rank, plane = at.rank, at.plane
    base = (rank // HALF) * HALF
    me = rank - base
    half_x = lax.rem(at.x, 2)

    barrier = pltpu.get_barrier_semaphore()

    def greet(device):
        pl.semaphore_signal(barrier, inc=1, device_id=device, device_id_type=MESH)

    def greet_half(step, carry):
        greet((plane, base + lax.rem(me + step, HALF)))
        return carry

    column = at.x * CORES + at.core

    def on_x(i):
        return at.device(x=i // CORES, core=lax.rem(i, CORES))

    def greet_x(step, carry):
        greet(on_x(lax.rem(column + step, XS * CORES)))
        return carry

    def greet_z(step, carry):
        greet(at.device(plane=lax.rem(plane + step, at.planes)))
        return carry

    lax.fori_loop(1, HALF, greet_half, 0)
    lax.fori_loop(1, XS * CORES, greet_x, 0)
    lax.fori_loop(1, at.planes, greet_z, 0)

    for load in loads:
        load.wait()

    own = weights.at[at.x, at.y * CORES + at.core]
    width = space_qkv.shape[-1]

    def padded(*parts):
        rows = sum(p.shape[0] for p in parts)
        parts = [p.astype(f32) for p in parts] + [jnp.zeros((16 - rows, width), f32)] * (rows < 16)
        return jnp.concatenate(parts, axis=0).astype(bf16)

    own[SPACE_QKV] = space_qkv[0:16, :]
    own[SPACE_QKV + 1] = padded(space_qkv[16:27, :])
    own[OUT_PIECE] = padded(space_out[...], time_out[0:LOW, :])
    own[TIME_QKV] = time_qkv[0:16, :]
    own[TIME_QKV + 1] = padded(time_qkv[16:27, :], time_out[LOW:PIECE, :])

    pl.semaphore_wait(barrier, HALF - 1 + XS * CORES - 1 + at.planes - 1)

    mine = 1 - lax.rem(plane, 2)
    other = 1 - mine
    gather = Gather(at, weights)

    def sib(k):
        return sib_sent.at[k], sib_recv.at[k]

    def pair(first, i):
        return gather.y_first(
            first + mine, recv.at[i], sent.at[i], sib(i), first + other, recv.at[i + 1], sent.at[i + 1], sib(i + 1)
        )

    space_steps = pair(SPACE_QKV, 0) + gather.x_first(OUT_PIECE, recv.at[2], sent.at[2], sib(2))
    time_steps = pair(TIME_QKV, 3)
    time_left = list(range(SPACE_DONE - TIME_AFTER, SPACE_DONE))

    def drain():
        gather.y_first_drain(sent.at[0], sent.at[1])
        gather.x_first_drain(sent.at[2])
        gather.y_first_drain(sent.at[3], sent.at[4])
        for k in range(PIECES):
            gather.sibling_wait(sib_sent.at[k])

    def run(steps, time):
        for action in steps_at(steps, time):
            action()

    def run_next():
        if time_left:
            run(time_steps, time_left.pop(0))

    def arrived(i):
        gather.sibling_wait(sib_recv.at[i])

    def slabs_start(i, src, dst):
        for dy in (4, 3, -3, 2, -2, 1, -1, 0):
            for across in (1, 0):
                for dcore in (1, 0):
                    if dy or across or dcore:
                        x = lax.rem(half_x + across, 2)
                        core = lax.rem(at.core + dcore, 2)
                        peer = (x * YS + at.dy(dy)) * CORES + core
                        pltpu.make_async_remote_copy(
                            src_ref=src.at[peer],
                            dst_ref=dst.at[me],
                            send_sem=slab_send.at[i],
                            recv_sem=slab_recv.at[i],
                            device_id=(plane, base + peer),
                            device_id_type=MESH,
                        ).start()

        own = pltpu.make_async_copy(src.at[me], dst.at[me], slab_own.at[i])
        own.start()
        own.wait()

    def slabs_wait(i, dst):
        wait_bytes(dst.at[pl.ds(0, HALF - 1)], slab_recv.at[i])

    def slabs_drain(i, src):
        wait_bytes(src.at[pl.ds(0, HALF - 1)], slab_send.at[i])

    clips = clip_scalars(frames, offsets, heights, widths)
    spread = spread_matrix()

    run(space_steps, 0)
    x = tokens[0].astype(f32)
    _, normed = normed_of(x, gain_row(space_gain))
    for t in range(1, SPACE_DONE):
        run(space_steps, t)
        run(time_steps, t - TIME_AFTER)
    arrived(0)
    arrived(1)
    count = jnp.int32(0)
    for first, last, size in clips:
        count = count + jnp.where((rank >= first) & (rank < last), size, 0)
    live_space = jnp.where(iota((FRAME, 1), 0) < count, 1.0, 0.0)
    mask_space = iota((FRAME, FRAME), 1) < count
    for g in range(8):
        project(normed, weights, SPACE_QKV, spread, qkv, g)
    blended = []
    for heads in head_groups():
        shares = shares_of(
            [qkv[:, head(h)] for h in heads], [qkv[:, head(8 + h)] for h in heads], mask_space, 1.0 - live_space
        )
        mixed = [dot_nn(p, qkv[:, head(16 + h)]) for p, h in zip(shares, heads)]
        for h, p, m in zip(heads, shares, mixed):
            share[h] = p
            blended.append((m * live_space).astype(bf16))
    run_next()
    arrived(2)
    hidden = (x + dot_nn(jnp.concatenate(blended, axis=1), piece_rows(weights, OUT_PIECE))).astype(bf16)
    hidden_ref[...] = hidden
    hidden_out[...] = hidden.reshape(hidden_out.shape)
    slabs_start(0, hidden_out, hidden_in)
    while time_left:
        run_next()
    arrived(3)
    arrived(4)
    back = time_out_back(cotangent[0], weights).astype(bf16)
    back_out[...] = back.reshape(back_out.shape)
    slabs_start(1, back_out, back_in)

    def tables(shape, dim):
        place = iota(shape, dim)
        tile = base + (place >> 2)
        slot = me * SLOTS + (place & 3)
        ident = jnp.zeros(shape, jnp.int32)
        begin = jnp.zeros(shape, jnp.int32)
        size_of = jnp.zeros(shape, jnp.int32)
        for c, (first, last, size) in enumerate(clips):
            member = (tile >= first) & (tile < last)
            ident = jnp.where(member, c + 1, ident)
            begin = jnp.where(member, first, begin)
            size_of = jnp.where(member, size, size_of)
        time = jnp.where(ident > 0, tile - begin, 0)
        return ident * 4 + (place & 3), time.astype(f32), slot < size_of

    key_q, time, live_q = tables((FRAME, 1), 0)
    key_k, _, live_k = tables((1, FRAME), 1)
    mask = (key_q == key_k) & live_k
    live = jnp.where(live_q, 1.0, 0.0)
    lane = iota((1, LANES), 1)
    pair = ((lane & 63) >> 4) * PIECE + (lane & 15)
    frequency = jnp.exp(pair.astype(f32) * (-math.log(ROPE_BASE) / (HEAD_SIZE // 2)))
    angle = time * frequency
    cosine = jnp.cos(angle)
    sine = jnp.where(lane < 64, -1.0, 1.0) * jnp.sin(angle)

    slabs_wait(0, hidden_in)
    x_time = hidden_in[...].astype(f32).reshape(FRAME, hidden_in.shape[-1])
    r_time, normed = normed_of(x_time, gain_row(time_gain))
    for g in range(8):
        project(normed, weights, TIME_QKV, spread, time_q, g)
    def turned(v):
        v = v.astype(f32)
        return (v * cosine + pltpu.roll(v, 64, 1) * sine).astype(bf16)

    def turned_back(v):
        v = v.astype(f32)
        return (v * cosine - pltpu.roll(v, 64, 1) * sine).astype(bf16)

    blended = []
    for heads in head_groups():
        queries = [turned(time_q[:, head(h)]) for h in heads]
        keys = [turned(time_q[:, head(8 + h)]) for h in heads]
        shares = shares_of(queries, keys, mask, 1.0 - live)
        mixed = [dot_nn(p, time_q[:, head(16 + h)]) for p, h in zip(shares, heads)]
        for h, q, k, p, m in zip(heads, queries, keys, shares, mixed):
            time_q[:, head(h)] = q
            time_q[:, head(8 + h)] = k
            time_share[h] = p
            blended.append((m * live).astype(bf16))
    blend_out[...] = jnp.concatenate(blended, axis=1).reshape(blend_out.shape)
    slabs_start(2, blend_out, blend_in)
    slabs_wait(1, back_in)
    grads = back_in[...].astype(f32).reshape(FRAME, back_in.shape[-1]) * live
    for heads in head_groups():
        dq, dk, dv = attend_back(
            [time_q[:, head(h)] for h in heads],
            [time_q[:, head(8 + h)] for h in heads],
            [time_q[:, head(16 + h)] for h in heads],
            [time_share[h] for h in heads],
            [grads[:, head(h)].astype(bf16) for h in heads],
        )
        dq, dk = [turned_back(v) for v in dq], [turned_back(v) for v in dk]
        for i, h in enumerate(heads):
            time_q[:, head(h)] = dq[i]
            time_q[:, head(8 + h)] = dk[i]
            time_q[:, head(16 + h)] = dv[i]
    dn = project_back(time_q, weights, TIME_QKV, spread).astype(bf16).astype(f32)
    front, d_time_gain = norm_back(x_time, r_time, gain_row(time_gain), dn)
    front_out[...] = front.reshape(front_out.shape)
    slabs_start(3, front_out, front_in)

    slabs_wait(2, blend_in)
    blended = blend_in[...].reshape(FRAME, blend_in.shape[-1])
    out_ref[0] = (hidden_ref[...].astype(f32) + time_out_forward(blended, weights)).astype(bf16)

    slabs_wait(3, front_in)
    front = front_in[...].astype(f32).reshape(FRAME, front_in.shape[-1])
    d_hidden = (cotangent[0].astype(f32) + front).astype(bf16)
    d_blended = (dot_nt(d_hidden, piece_rows(weights, OUT_PIECE)).astype(bf16).astype(f32) * live_space).astype(bf16)
    for heads in head_groups():
        dq, dk, dv = attend_back(
            [qkv[:, head(h)] for h in heads],
            [qkv[:, head(8 + h)] for h in heads],
            [qkv[:, head(16 + h)] for h in heads],
            [share[h] for h in heads],
            [d_blended[:, head(h)] for h in heads],
        )
        for i, h in enumerate(heads):
            qkv[:, head(h)] = dq[i]
            qkv[:, head(8 + h)] = dk[i]
            qkv[:, head(16 + h)] = dv[i]
    dn = project_back(qkv, weights, SPACE_QKV, spread).astype(bf16).astype(f32)
    x = tokens[0].astype(f32)
    r, _ = normed_of(x, gain_row(space_gain))
    dx, d_space_gain = norm_back(x, r, gain_row(space_gain), dn)

    def reduce(i, size, mine, held, to):
        held[mine] = sums[i]

        def step(k, carry):
            pltpu.make_async_remote_copy(
                src_ref=sums.at[i],
                dst_ref=held.at[mine],
                send_sem=sum_send.at[i],
                recv_sem=sum_recv.at[i],
                device_id=to(lax.rem(mine + k, size)),
                device_id_type=MESH,
            ).start()
            return carry

        lax.fori_loop(1, size, step, 0)

    def reduced(i, size, held):
        if size > 1:
            wait_bytes(held.at[pl.ds(0, size - 1)], sum_recv.at[i])
        total = held[0]
        for k in range(1, size):
            total = total + held[k]
        return total

    sums[0, 0:1] = d_space_gain
    sums[0, 1:2] = d_time_gain
    reduce(0, XS * CORES, column, sums_x, on_x)
    grad_ref[0] = (d_hidden.astype(f32) + dx.astype(f32)).astype(bf16)
    total = reduced(0, XS * CORES, sums_x)
    sums[1] = total
    reduce(1, YS, at.y, sums_y, lambda i: at.device(y=i))
    for i, src in ((0, hidden_out), (1, back_out), (2, blend_out), (3, front_out)):
        slabs_drain(i, src)
    total = reduced(1, YS, sums_y)
    sums[2] = total
    reduce(2, at.planes, plane, sums_z, lambda i: at.device(plane=i))
    drain()
    total = reduced(2, at.planes, sums_z)
    for i, size, held in ((0, XS * CORES, sums_x), (1, YS, sums_y), (2, at.planes, sums_z)):
        if size > 1:
            wait_bytes(held.at[pl.ds(0, size - 1)], sum_send.at[i])
    gains_ref[...] = total * (1.0 / math.sqrt(at.planes * XS * YS * CORES * FRAME))


VMEM_SPEC = pl.BlockSpec(memory_space=pltpu.VMEM)
HBM_SPEC = pl.BlockSpec(memory_space=pltpu.HBM)
LIMIT = 56 * 1024 * 1024


def shards(
    tokens,
    cotangent,
    clip_frames,
    clip_offsets,
    clip_heights,
    clip_widths,
    spatial_gain,
    spatial_qkv,
    spatial_out,
    temporal_gain,
    temporal_qkv,
    temporal_out,
):
    width = tokens.shape[2]
    inner = HEADS * LANES
    planes = lax.axis_size("dp")
    dma = pltpu.SemaphoreType.DMA

    def slab(columns):
        return pltpu.VMEM((HALF, SLOTS, columns), bf16)

    gather_sems = [dma((PIECES, 31)), dma((PIECES, 3)), dma((PIECES,)), dma((PIECES,))]
    operands = (
        clip_frames,
        clip_offsets,
        clip_heights,
        clip_widths,
        tokens,
        cotangent,
        spatial_gain,
        spatial_qkv,
        spatial_out,
        temporal_gain,
        temporal_qkv,
        temporal_out,
    )
    loaded = [pltpu.SMEM(a.shape, a.dtype) for a in operands[:4]]
    loaded += [pltpu.VMEM(a.shape, a.dtype) for a in operands[4:]]
    return pl.pallas_call(
        whole,
        out_shape=[
            jax.ShapeDtypeStruct(tokens.shape, bf16),
            jax.ShapeDtypeStruct(tokens.shape, bf16),
            jax.ShapeDtypeStruct((2, width), f32),
        ],
        in_specs=[HBM_SPEC] * 12,
        out_specs=[VMEM_SPEC] * 3,
        scratch_shapes=loaded
        + [
            pltpu.VMEM((XS, YS * CORES, PIECES, 16, width), bf16),
            pltpu.VMEM((FRAME, 3 * inner), bf16),
            pltpu.VMEM((FRAME, 3 * inner), bf16),
            pltpu.VMEM((HEADS, FRAME, FRAME), bf16),
            pltpu.VMEM((HEADS, FRAME, FRAME), bf16),
            pltpu.VMEM((FRAME, width), bf16),
            slab(width),
            slab(width),
            slab(inner),
            slab(inner),
            slab(inner),
            slab(inner),
            slab(width),
            slab(width),
            pltpu.VMEM((3, 2, width), f32),
            pltpu.VMEM((XS * CORES, 2, width), f32),
            pltpu.VMEM((YS, 2, width), f32),
            pltpu.VMEM((planes, 2, width), f32),
        ]
        + gather_sems
        + [dma((4,)), dma((4,)), dma((4,)), dma((3,)), dma((3,)), dma((12,))],
        compiler_params=pltpu.CompilerParams(
            collective_id=0, has_side_effects=True, vmem_limit_bytes=LIMIT
        ),
    )(*operands)


def solution(mesh):
    return jax.shard_map(
        shards,
        mesh=mesh,
        in_specs=(
            P("dp", "ctx", None),
            P("dp", "ctx", None),
            P("dp", None),
            P("dp", None),
            P("dp", None),
            P("dp", None),
            P(),
            P("ctx", None),
            P("ctx", None),
            P(),
            P("ctx", None),
            P("ctx", None),
        ),
        out_specs=(P("dp", "ctx", None), P("dp", "ctx", None), P()),
        check_vma=False,
    )
```

```python
import math

import jax
import jax.numpy as jnp
from jax import lax
from jax.experimental import pallas as pl
from jax.experimental.pallas import tpu as pltpu
from jax.sharding import PartitionSpec as P

HEADS = 8
FRAME = 128
LANES = 128
EPSILON = 1e-06
ROPE_BASE = 10000.0
HEAD_SIZE = 72
PIECE = 9
PIECE_PAD = 16
QKV_PAD = 32
GROUP = 256
GROUP_HEADS = 3 * LANES
HALF = 32
bf16 = jnp.bfloat16
f32 = jnp.float32
MESH = pl.DeviceIdType.MESH


def dot_nn(a, b):
    return lax.dot_general(a, b, (((1,), (0,)), ((), ())), preferred_element_type=f32)


def dot_nt(a, b):
    return lax.dot_general(a, b, (((1,), (1,)), ((), ())), preferred_element_type=f32)


def dot_tn(a, b):
    return lax.dot_general(a, b, (((0,), (0,)), ((), ())), preferred_element_type=f32)


def iota(shape, dim):
    return lax.broadcasted_iota(jnp.int32, shape, dim)


def spread_matrix():
    lane = iota((GROUP, GROUP_HEADS), 1)
    row = iota((GROUP, GROUP_HEADS), 0)
    block = lane >> 4
    within = lane & 15
    third = ((block * 11) >> 5)
    source = third * QKV_PAD + (block - 3 * third) * PIECE + within
    return jnp.where((row == source) & (within < PIECE), 1.0, 0.0).astype(bf16)


def normed_of(x, gain):
    r = lax.rsqrt(jnp.mean(x * x, axis=-1, keepdims=True) + EPSILON)
    return r, (x * r * gain).astype(bf16)


def norm_back(x, r, gain, dn):
    d_gain = jnp.sum(dn * (x * r), axis=0, keepdims=True)
    u = dn * gain
    inner = jnp.sum(u * x, axis=-1, keepdims=True) * (1.0 / x.shape[-1])
    return (r * u - x * (r * r * r * inner)).astype(bf16), d_gain


PIECES = 5
SPACE_QKV, OUT_PIECE, TIME_QKV = 0, 2, 3
LOW, HIGH_AT = 7, 11


def qkv_rows(weights, first, g):
    half = slice(8 * (g % 2), 8 * (g % 2) + 8)
    return weights[g // 2, half, first : first + 2].reshape(GROUP, weights.shape[-1])


def project(normed, weights, first, spread, into, g):
    part = dot_nt(normed, qkv_rows(weights, first, g)).astype(bf16)
    into[:, g * GROUP_HEADS : (g + 1) * GROUP_HEADS] = dot_nn(part, spread).astype(bf16)


def project_back(grads, weights, first, spread):
    parts = [
        dot_nt(grads[:, g * GROUP_HEADS : (g + 1) * GROUP_HEADS], spread).astype(bf16) for g in range(8)
    ]
    rows = weights[:, :, first : first + 2].reshape(8 * GROUP, weights.shape[-1])
    return dot_nn(jnp.concatenate(parts, axis=1), rows)


def piece_rows(weights, piece):
    return weights[:, :, piece].reshape(HEADS * LANES, weights.shape[-1])


def by_head(values, change):
    return jnp.concatenate([change(values[:, head(h)]) for h in range(HEADS)], axis=1)


def time_out_forward(blended, weights):
    within = iota((1, LANES), 1) & 15
    wide = blended.astype(f32)
    low = by_head(wide, lambda v: jnp.where(within >= PIECE, pltpu.roll(v, PIECE, 1), 0.0)).astype(bf16)
    is_high = (within >= HIGH_AT) & (within < HIGH_AT + PIECE - LOW)
    high = by_head(wide, lambda v: jnp.where(is_high, pltpu.roll(v, HIGH_AT - LOW, 1), 0.0)).astype(bf16)
    return dot_nn(low, piece_rows(weights, OUT_PIECE)) + dot_nn(high, piece_rows(weights, TIME_QKV + 1))


def time_out_back(grads, weights):
    within = iota((1, LANES), 1) & 15
    low = by_head(dot_nt(grads, piece_rows(weights, OUT_PIECE)), lambda v: pltpu.roll(v, LANES - PIECE, 1))
    high = by_head(
        dot_nt(grads, piece_rows(weights, TIME_QKV + 1)), lambda v: pltpu.roll(v, LANES - (HIGH_AT - LOW), 1)
    )
    within = jnp.concatenate([within] * HEADS, axis=1)
    return jnp.where(within < LOW, low, jnp.where(within < PIECE, high, 0.0))


SCALE = HEAD_SIZE ** (-0.5)


def shares_of(queries, keys, mask, dead):
    scores = [dot_nt(q, k) for q, k in zip(queries, keys)]
    weights = [jnp.where(mask, jnp.exp(s * SCALE), 0.0) for s in scores]
    totals = [jnp.sum(w, axis=-1, keepdims=True) + dead for w in weights]
    return [(w / t).astype(bf16) for w, t in zip(weights, totals)]


def attend_back(queries, keys, values, shares, grads):
    ds = [dot_nt(g, v).astype(bf16).astype(f32) for g, v in zip(grads, values)]
    dv = [dot_tn(p, g).astype(bf16) for p, g in zip(shares, grads)]
    wide = [p.astype(f32) for p in shares]
    inner = [jnp.sum(d * p, axis=-1, keepdims=True) for d, p in zip(ds, wide)]
    d = [(p * (x - c) * SCALE).astype(bf16) for p, x, c in zip(wide, ds, inner)]
    dq = [dot_nn(x, k).astype(bf16) for x, k in zip(d, keys)]
    dk = [dot_tn(x, q).astype(bf16) for x, q in zip(d, queries)]
    return dq, dk, dv


TOGETHER = 8


def head_groups():
    return [range(h, h + TOGETHER) for h in range(0, HEADS, TOGETHER)]


def head(h):
    return slice(h * LANES, (h + 1) * LANES)


def clip_scalars(frames, offsets, heights, widths):
    out = []
    for c in range(8):
        start = offsets[0, c] >> 7
        out.append((start, start + frames[0, c], heights[0, c] * widths[0, c]))
    return out


XS, YS, CORES = 4, 8, 2
SPACE_DONE, TIME_AFTER = 8, 2
SLOTS = FRAME // HALF


def wait_bytes(ref, sem):
    pltpu.make_async_copy(ref, ref, sem).wait()


def gain_row(gain):
    return gain[...].reshape(1, gain.shape[0])


class Place:
    def __init__(self):
        self.plane = lax.axis_index("dp")
        self.planes = lax.axis_size("dp")
        self.rank = lax.axis_index("ctx")
        self.x = self.rank // (YS * CORES)
        self.y = lax.rem(self.rank // CORES, YS)
        self.core = lax.rem(self.rank, CORES)

    def device(self, x=None, y=None, core=None, plane=None):
        x = self.x if x is None else x
        y = self.y if y is None else y
        core = self.core if core is None else core
        plane = self.plane if plane is None else plane
        return (plane, (x * YS + y) * CORES + core)

    def dx(self, step):
        return lax.rem(self.x + step + XS, XS)

    def dy(self, step):
        return lax.rem(self.y + step + YS, YS)

    def dz(self, step):
        return lax.rem(self.plane + step + self.planes, self.planes)


class Gather:
    def __init__(self, at, weights):
        self.at = at
        self.weights = weights
        self.up, self.down = at.device(y=at.dy(1)), at.device(y=at.dy(-1))
        self.right, self.left = at.device(x=at.dx(1)), at.device(x=at.dx(-1))
        self.above, self.below = at.device(plane=at.dz(1)), at.device(plane=at.dz(-1))

    def block(self, x, y, piece):
        return self.weights.at[x, y * CORES + self.at.core, piece]

    def x_of(self, kind):
        return (self.at.x, self.at.dx(-1), self.at.dx(1), self.at.dx(2))[kind]

    def send(self, ref, device, send_sem, recv_sem):
        pltpu.make_async_remote_copy(
            src_ref=ref, dst_ref=ref, send_sem=send_sem, recv_sem=recv_sem, device_id=device, device_id_type=MESH
        ).start()

    def sibling(self, y, piece, sems):
        at = self.at
        ref = self.weights.at[:, y * CORES + at.core, piece]
        self.send(ref, at.device(core=1 - at.core), sems[0], sems[1])

    def sibling_wait(self, sem):
        wait_bytes(self.weights.at[:, 0:8, 0], sem)

    def y_first(self, piece, recv, sent, sib, other=None, z_recv=None, z_sent=None, z_sib=None):
        at = self.at
        steps = []

        def y_of(j):
            return at.dy(-j) if j <= 4 else at.dy(j - 4)

        def ident(kind, j):
            return j - 1 if kind == 0 else 7 + (kind - 1) * 8 + j

        def over_z(kind, j):
            if other is not None:
                i = ident(kind, j)
                ref = self.block(self.x_of(kind), y_of(j), piece)
                self.send(ref, self.above if i % 2 == 0 else self.below, z_sent.at[i % 2], z_recv.at[i])

        def along_y(j, what, sems, come):
            ref = self.block(at.x, y_of(j), what)
            if j > 0:
                wait_bytes(ref, come.at[ident(0, j)])
            if j in (0, 1, 2, 3):
                self.send(ref, self.up, sems, come.at[ident(0, j + 1)])
            if j in (0, 5, 6):
                self.send(ref, self.down, sems, come.at[ident(0, 5 if j == 0 else j + 1)])

        plus = (0, 1, 2, 3)

        def arrive_y(j):
            along_y(j, piece, sent.at[0], recv)
            ref = self.block(at.x, y_of(j), piece)
            self.send(ref, self.right, sent.at[1], recv.at[ident(1, j)])
            self.send(ref, self.left, sent.at[1], recv.at[ident(2, j)])
            if other is not None:
                along_y(j, other, z_sent.at[2], z_recv)

        def arrive_x(kind, j):
            ref = self.block(self.x_of(kind), y_of(j), piece)
            wait_bytes(ref, recv.at[ident(kind, j)])
            if kind == 1 and j in plus:
                self.send(ref, self.right, sent.at[1], recv.at[ident(3, j)])
            if kind == 2 and j not in plus:
                self.send(ref, self.left, sent.at[1], recv.at[ident(3, j)])
            over_z(kind, j)

        def arrive_z(j):
            for kind in (1, 2, 3):
                wait_bytes(self.block(self.x_of(kind), y_of(j), other), z_recv.at[ident(kind, j)])
            self.sibling(y_of(j), other, z_sib)

        for j in range(8):
            far = j if j <= 4 else j - 4
            steps.append((far, 0, lambda j=j: arrive_y(j)))
            for kind in (1, 2, 3):
                steps.append((far + (1 if kind < 3 else 2), 1, lambda kind=kind, j=j: arrive_x(kind, j)))
            steps.append((far + 2, 3, lambda j=j: self.sibling(y_of(j), piece, sib)))
            if other is not None:
                steps.append((far + 3, 2, lambda j=j: arrive_z(j)))
        return steps

    def y_first_drain(self, sent, z_sent=None):
        wait_bytes(self.weights.at[0, 0:7, 0], sent.at[0])
        wait_bytes(self.weights.at[0:3, 0:8, 0], sent.at[1])
        if z_sent is not None:
            wait_bytes(self.weights.at[0, 0:12, 0], z_sent.at[0])
            wait_bytes(self.weights.at[0, 0:12, 0], z_sent.at[1])
            wait_bytes(self.weights.at[0, 0:7, 0], z_sent.at[2])

    def x_first(self, piece, recv, sent, sib):
        at = self.at
        steps = []

        def y_of(j):
            return at.dy(-j) if j <= 3 else at.dy(j - 3)

        def number(kind, j):
            return kind - 1 if j == 0 else 3 + kind * 7 + j - 1

        def come(kind, j):
            ref = self.block(self.x_of(kind), y_of(j), piece)
            if kind > 0 or j > 0:
                wait_bytes(ref, recv.at[number(kind, j)])
            if j == 0 and kind == 0:
                self.send(ref, self.right, sent.at[0], recv.at[number(1, 0)])
                self.send(ref, self.left, sent.at[0], recv.at[number(2, 0)])
            if j == 0 and kind == 2:
                self.send(ref, self.left, sent.at[0], recv.at[number(3, 0)])
            if j in (0, 1, 2):
                self.send(ref, self.up, sent.at[1], recv.at[number(kind, j + 1)])
            if j in (0, 4, 5, 6):
                self.send(ref, self.down, sent.at[1], recv.at[number(kind, 4 if j == 0 else j + 1)])

        for j in range(8):
            far = j if j <= 3 else j - 3
            for kind in range(4):
                steps.append((far + (0, 1, 1, 2)[kind], 1.5, lambda kind=kind, j=j: come(kind, j)))
            steps.append((far + 2, 3, lambda j=j: self.sibling(y_of(j), piece, sib)))
        return steps

    def x_first_drain(self, sent):
        wait_bytes(self.weights.at[0, 0:3, 0], sent.at[0])
        wait_bytes(self.weights.at[:, 0:7, 0], sent.at[1])


def steps_at(steps, time):
    return [action for t, _, action in sorted(steps, key=lambda step: step[1]) if t == time]


def whole(
    *refs,
):
    operands, loaded = refs[:12], refs[15:27]
    loads = [
        pltpu.make_async_copy(src, dst, refs[-1].at[i]) for i, (src, dst) in enumerate(zip(operands, loaded))
    ]
    for load in loads:
        load.start()
    whole_loaded(loads, *loaded, *refs[12:15], *refs[27:-1])


def whole_loaded(
    loads,
    frames,
    offsets,
    heights,
    widths,
    tokens,
    cotangent,
    space_gain,
    space_qkv,
    space_out,
    time_gain,
    time_qkv,
    time_out,
    out_ref,
    grad_ref,
    gains_ref,
    weights,
    qkv,
    time_q,
    share,
    time_share,
    hidden_ref,
    hidden_out,
    hidden_in,
    back_out,
    back_in,
    blend_out,
    blend_in,
    front_out,
    front_in,
    sums,
    sums_x,
    sums_y,
    sums_z,
    *sems,
):
    recv, sent, sib_sent, sib_recv, slab_send, slab_recv, slab_own, sum_send, sum_recv = sems
    at = Place()
    rank, plane = at.rank, at.plane
    base = (rank // HALF) * HALF
    me = rank - base
    half_x = lax.rem(at.x, 2)

    barrier = pltpu.get_barrier_semaphore()

    def greet(device):
        pl.semaphore_signal(barrier, inc=1, device_id=device, device_id_type=MESH)

    def greet_half(step, carry):
        greet((plane, base + lax.rem(me + step, HALF)))
        return carry

    column = at.x * CORES + at.core

    def on_x(i):
        return at.device(x=i // CORES, core=lax.rem(i, CORES))

    def greet_x(step, carry):
        greet(on_x(lax.rem(column + step, XS * CORES)))
        return carry

    def greet_z(step, carry):
        greet(at.device(plane=lax.rem(plane + step, at.planes)))
        return carry

    lax.fori_loop(1, HALF, greet_half, 0)
    lax.fori_loop(1, XS * CORES, greet_x, 0)
    lax.fori_loop(1, at.planes, greet_z, 0)

    for load in loads:
        load.wait()

    own = weights.at[at.x, at.y * CORES + at.core]
    width = space_qkv.shape[-1]

    def padded(*parts):
        rows = sum(p.shape[0] for p in parts)
        parts = [p.astype(f32) for p in parts] + [jnp.zeros((16 - rows, width), f32)] * (rows < 16)
        return jnp.concatenate(parts, axis=0).astype(bf16)

    own[SPACE_QKV] = space_qkv[0:16, :]
    own[SPACE_QKV + 1] = padded(space_qkv[16:27, :])
    own[OUT_PIECE] = padded(space_out[...], time_out[0:LOW, :])
    own[TIME_QKV] = time_qkv[0:16, :]
    own[TIME_QKV + 1] = padded(time_qkv[16:27, :], time_out[LOW:PIECE, :])

    pl.semaphore_wait(barrier, HALF - 1 + XS * CORES - 1 + at.planes - 1)

    mine = 1 - lax.rem(plane, 2)
    other = 1 - mine
    gather = Gather(at, weights)

    def sib(k):
        return sib_sent.at[k], sib_recv.at[k]

    def pair(first, i):
        return gather.y_first(
            first + mine, recv.at[i], sent.at[i], sib(i), first + other, recv.at[i + 1], sent.at[i + 1], sib(i + 1)
        )

    space_steps = pair(SPACE_QKV, 0) + gather.x_first(OUT_PIECE, recv.at[2], sent.at[2], sib(2))
    time_steps = pair(TIME_QKV, 3)
    time_left = list(range(SPACE_DONE - TIME_AFTER, SPACE_DONE))

    def drain():
        gather.y_first_drain(sent.at[0], sent.at[1])
        gather.x_first_drain(sent.at[2])
        gather.y_first_drain(sent.at[3], sent.at[4])
        for k in range(PIECES):
            gather.sibling_wait(sib_sent.at[k])

    def run(steps, time):
        for action in steps_at(steps, time):
            action()

    def run_next():
        if time_left:
            run(time_steps, time_left.pop(0))

    def arrived(i):
        gather.sibling_wait(sib_recv.at[i])

    def slabs_start(i, src, dst):
        for dy in (4, 3, -3, 2, -2, 1, -1, 0):
            for across in (1, 0):
                for dcore in (1, 0):
                    if dy or across or dcore:
                        x = lax.rem(half_x + across, 2)
                        core = lax.rem(at.core + dcore, 2)
                        peer = (x * YS + at.dy(dy)) * CORES + core
                        pltpu.make_async_remote_copy(
                            src_ref=src.at[peer],
                            dst_ref=dst.at[me],
                            send_sem=slab_send.at[i],
                            recv_sem=slab_recv.at[i],
                            device_id=(plane, base + peer),
                            device_id_type=MESH,
                        ).start()

        own = pltpu.make_async_copy(src.at[me], dst.at[me], slab_own.at[i])
        own.start()
        own.wait()

    def slabs_wait(i, dst):
        wait_bytes(dst.at[pl.ds(0, HALF - 1)], slab_recv.at[i])

    def slabs_drain(i, src):
        wait_bytes(src.at[pl.ds(0, HALF - 1)], slab_send.at[i])

    clips = clip_scalars(frames, offsets, heights, widths)
    spread = spread_matrix()

    run(space_steps, 0)
    x = tokens[0].astype(f32)
    _, normed = normed_of(x, gain_row(space_gain))
    for t in range(1, SPACE_DONE):
        run(space_steps, t)
        run(time_steps, t - TIME_AFTER)
    arrived(0)
    arrived(1)
    count = jnp.int32(0)
    for first, last, size in clips:
        count = count + jnp.where((rank >= first) & (rank < last), size, 0)
    live_space = jnp.where(iota((FRAME, 1), 0) < count, 1.0, 0.0)
    mask_space = iota((FRAME, FRAME), 1) < count
    for g in range(8):
        project(normed, weights, SPACE_QKV, spread, qkv, g)
    blended = []
    for heads in head_groups():
        shares = shares_of(
            [qkv[:, head(h)] for h in heads], [qkv[:, head(8 + h)] for h in heads], mask_space, 1.0 - live_space
        )
        mixed = [dot_nn(p, qkv[:, head(16 + h)]) for p, h in zip(shares, heads)]
        for h, p, m in zip(heads, shares, mixed):
            share[h] = p
            blended.append((m * live_space).astype(bf16))
    run_next()
    arrived(2)
    hidden = (x + dot_nn(jnp.concatenate(blended, axis=1), piece_rows(weights, OUT_PIECE))).astype(bf16)
    hidden_ref[...] = hidden
    hidden_out[...] = hidden.reshape(hidden_out.shape)
    slabs_start(0, hidden_out, hidden_in)
    while time_left:
        run_next()
    arrived(3)
    arrived(4)
    back = time_out_back(cotangent[0], weights).astype(bf16)
    back_out[...] = back.reshape(back_out.shape)
    slabs_start(1, back_out, back_in)

    def tables(shape, dim):
        place = iota(shape, dim)
        tile = base + (place >> 2)
        slot = me * SLOTS + (place & 3)
        ident = jnp.zeros(shape, jnp.int32)
        begin = jnp.zeros(shape, jnp.int32)
        size_of = jnp.zeros(shape, jnp.int32)
        for c, (first, last, size) in enumerate(clips):
            member = (tile >= first) & (tile < last)
            ident = jnp.where(member, c + 1, ident)
            begin = jnp.where(member, first, begin)
            size_of = jnp.where(member, size, size_of)
        time = jnp.where(ident > 0, tile - begin, 0)
        return ident * 4 + (place & 3), time.astype(f32), slot < size_of

    key_q, time, live_q = tables((FRAME, 1), 0)
    key_k, _, live_k = tables((1, FRAME), 1)
    mask = (key_q == key_k) & live_k
    live = jnp.where(live_q, 1.0, 0.0)
    lane = iota((1, LANES), 1)
    pair = ((lane & 63) >> 4) * PIECE + (lane & 15)
    frequency = jnp.exp(pair.astype(f32) * (-math.log(ROPE_BASE) / (HEAD_SIZE // 2)))
    angle = time * frequency
    cosine = jnp.cos(angle)
    sine = jnp.where(lane < 64, -1.0, 1.0) * jnp.sin(angle)

    slabs_wait(0, hidden_in)
    x_time = hidden_in[...].astype(f32).reshape(FRAME, hidden_in.shape[-1])
    r_time, normed = normed_of(x_time, gain_row(time_gain))
    for g in range(8):
        project(normed, weights, TIME_QKV, spread, time_q, g)
    def turned(v):
        v = v.astype(f32)
        return (v * cosine + pltpu.roll(v, 64, 1) * sine).astype(bf16)

    def turned_back(v):
        v = v.astype(f32)
        return (v * cosine - pltpu.roll(v, 64, 1) * sine).astype(bf16)

    blended = []
    for heads in head_groups():
        queries = [turned(time_q[:, head(h)]) for h in heads]
        keys = [turned(time_q[:, head(8 + h)]) for h in heads]
        shares = shares_of(queries, keys, mask, 1.0 - live)
        mixed = [dot_nn(p, time_q[:, head(16 + h)]) for p, h in zip(shares, heads)]
        for h, q, k, p, m in zip(heads, queries, keys, shares, mixed):
            time_q[:, head(h)] = q
            time_q[:, head(8 + h)] = k
            time_share[h] = p
            blended.append((m * live).astype(bf16))
    blend_out[...] = jnp.concatenate(blended, axis=1).reshape(blend_out.shape)
    slabs_wait(1, back_in)
    grads = back_in[...].astype(f32).reshape(FRAME, back_in.shape[-1]) * live
    for heads in head_groups():
        dq, dk, dv = attend_back(
            [time_q[:, head(h)] for h in heads],
            [time_q[:, head(8 + h)] for h in heads],
            [time_q[:, head(16 + h)] for h in heads],
            [time_share[h] for h in heads],
            [grads[:, head(h)].astype(bf16) for h in heads],
        )
        dq, dk = [turned_back(v) for v in dq], [turned_back(v) for v in dk]
        for i, h in enumerate(heads):
            time_q[:, head(h)] = dq[i]
            time_q[:, head(8 + h)] = dk[i]
            time_q[:, head(16 + h)] = dv[i]
    dn = project_back(time_q, weights, TIME_QKV, spread).astype(bf16).astype(f32)
    front, d_time_gain = norm_back(x_time, r_time, gain_row(time_gain), dn)
    front_out[...] = front.reshape(front_out.shape)
    slabs_start(3, front_out, front_in)
    slabs_start(2, blend_out, blend_in)

    slabs_wait(3, front_in)
    front = front_in[...].astype(f32).reshape(FRAME, front_in.shape[-1])
    d_hidden = (cotangent[0].astype(f32) + front).astype(bf16)
    d_blended = (dot_nt(d_hidden, piece_rows(weights, OUT_PIECE)).astype(bf16).astype(f32) * live_space).astype(bf16)
    for heads in head_groups():
        dq, dk, dv = attend_back(
            [qkv[:, head(h)] for h in heads],
            [qkv[:, head(8 + h)] for h in heads],
            [qkv[:, head(16 + h)] for h in heads],
            [share[h] for h in heads],
            [d_blended[:, head(h)] for h in heads],
        )
        for i, h in enumerate(heads):
            qkv[:, head(h)] = dq[i]
            qkv[:, head(8 + h)] = dk[i]
            qkv[:, head(16 + h)] = dv[i]
    dn = project_back(qkv, weights, SPACE_QKV, spread).astype(bf16).astype(f32)
    x = tokens[0].astype(f32)
    r, _ = normed_of(x, gain_row(space_gain))
    dx, d_space_gain = norm_back(x, r, gain_row(space_gain), dn)

    def reduce(i, size, mine, held, to):
        held[mine] = sums[i]

        def step(k, carry):
            pltpu.make_async_remote_copy(
                src_ref=sums.at[i],
                dst_ref=held.at[mine],
                send_sem=sum_send.at[i],
                recv_sem=sum_recv.at[i],
                device_id=to(lax.rem(mine + k, size)),
                device_id_type=MESH,
            ).start()
            return carry

        lax.fori_loop(1, size, step, 0)

    def reduced(i, size, held):
        if size > 1:
            wait_bytes(held.at[pl.ds(0, size - 1)], sum_recv.at[i])
        total = held[0]
        for k in range(1, size):
            total = total + held[k]
        return total

    sums[0, 0:1] = d_space_gain
    sums[0, 1:2] = d_time_gain
    reduce(0, XS * CORES, column, sums_x, on_x)
    grad_ref[0] = (d_hidden.astype(f32) + dx.astype(f32)).astype(bf16)

    slabs_wait(2, blend_in)
    blended = blend_in[...].reshape(FRAME, blend_in.shape[-1])
    output = (hidden_ref[...].astype(f32) + time_out_forward(blended, weights)).astype(bf16)
    out_ref[0] = output

    total = reduced(0, XS * CORES, sums_x)
    sums[1] = total
    reduce(1, YS, at.y, sums_y, lambda i: at.device(y=i))
    for i, src in ((0, hidden_out), (1, back_out), (2, blend_out), (3, front_out)):
        slabs_drain(i, src)
    total = reduced(1, YS, sums_y)
    sums[2] = total
    reduce(2, at.planes, plane, sums_z, lambda i: at.device(plane=i))
    drain()
    total = reduced(2, at.planes, sums_z)
    for i, size, held in ((0, XS * CORES, sums_x), (1, YS, sums_y), (2, at.planes, sums_z)):
        if size > 1:
            wait_bytes(held.at[pl.ds(0, size - 1)], sum_send.at[i])
    gains_ref[...] = total * (1.0 / math.sqrt(at.planes * XS * YS * CORES * FRAME))


VMEM_SPEC = pl.BlockSpec(memory_space=pltpu.VMEM)
HBM_SPEC = pl.BlockSpec(memory_space=pltpu.HBM)
LIMIT = 56 * 1024 * 1024


def shards(
    tokens,
    cotangent,
    clip_frames,
    clip_offsets,
    clip_heights,
    clip_widths,
    spatial_gain,
    spatial_qkv,
    spatial_out,
    temporal_gain,
    temporal_qkv,
    temporal_out,
):
    width = tokens.shape[2]
    inner = HEADS * LANES
    planes = lax.axis_size("dp")
    dma = pltpu.SemaphoreType.DMA

    def slab(columns):
        return pltpu.VMEM((HALF, SLOTS, columns), bf16)

    gather_sems = [dma((PIECES, 31)), dma((PIECES, 3)), dma((PIECES,)), dma((PIECES,))]
    operands = (
        clip_frames,
        clip_offsets,
        clip_heights,
        clip_widths,
        tokens,
        cotangent,
        spatial_gain,
        spatial_qkv,
        spatial_out,
        temporal_gain,
        temporal_qkv,
        temporal_out,
    )
    loaded = [pltpu.SMEM(a.shape, a.dtype) for a in operands[:4]]
    loaded += [pltpu.VMEM(a.shape, a.dtype) for a in operands[4:]]
    return pl.pallas_call(
        whole,
        out_shape=[
            jax.ShapeDtypeStruct(tokens.shape, bf16),
            jax.ShapeDtypeStruct(tokens.shape, bf16),
            jax.ShapeDtypeStruct((2, width), f32),
        ],
        in_specs=[HBM_SPEC] * 12,
        out_specs=[VMEM_SPEC] * 3,
        scratch_shapes=loaded
        + [
            pltpu.VMEM((XS, YS * CORES, PIECES, 16, width), bf16),
            pltpu.VMEM((FRAME, 3 * inner), bf16),
            pltpu.VMEM((FRAME, 3 * inner), bf16),
            pltpu.VMEM((HEADS, FRAME, FRAME), bf16),
            pltpu.VMEM((HEADS, FRAME, FRAME), bf16),
            pltpu.VMEM((FRAME, width), bf16),
            slab(width),
            slab(width),
            slab(inner),
            slab(inner),
            slab(inner),
            slab(inner),
            slab(width),
            slab(width),
            pltpu.VMEM((3, 2, width), f32),
            pltpu.VMEM((XS * CORES, 2, width), f32),
            pltpu.VMEM((YS, 2, width), f32),
            pltpu.VMEM((planes, 2, width), f32),
        ]
        + gather_sems
        + [dma((4,)), dma((4,)), dma((4,)), dma((3,)), dma((3,)), dma((12,))],
        compiler_params=pltpu.CompilerParams(
            collective_id=0, has_side_effects=True, vmem_limit_bytes=LIMIT
        ),
    )(*operands)


def solution(mesh):
    return jax.shard_map(
        shards,
        mesh=mesh,
        in_specs=(
            P("dp", "ctx", None),
            P("dp", "ctx", None),
            P("dp", None),
            P("dp", None),
            P("dp", None),
            P("dp", None),
            P(),
            P("ctx", None),
            P("ctx", None),
            P(),
            P("ctx", None),
            P("ctx", None),
        ),
        out_specs=(P("dp", "ctx", None), P("dp", "ctx", None), P()),
        check_vma=False,
    )
```
